32 devices in a mesh: axial: 8 (over z, core), circ: 4 (over y, x).
Axes of the slice: x: 2, y: 2, z: 4, core: 2. Of those that a mesh axis runs over, the one named last changes fastest.
Arguments:
- right_side: float32 [64, 64, 256], P('axial', 'circ'), may hold values from -6 to 6
- stiffness: float32 [64, 64, 256], P('axial', 'circ'), may hold values from 0.03 to 0.3
- material: int32 [64, 64, 256], P('axial', 'circ'), may hold values from 0 to 15
- groups: int32 [64, 64, 256], P('axial', 'circ'), may hold values from 0 to 7, as said below
Outputs:
- solution: float32 [64, 64, 256], P('axial', 'circ')
- residual: float32 [64, 64, 256], P('axial', 'circ')
The draws below stay inside these ranges and needn't reach their ends.
Inputs may be any that keep to these rules, and one draw needn't show every extreme that they name: `groups`: in every column of cells along the third dimension every group number from 0 to 7 occurs.
All inputs are finite; a program needn't handle non-finite values.
Results may differ from the reference program's by a relative error of at most 0.0003.
Values sent between devices are 32-bit elements; how exact they have to be, the bound alone decides.
A program may use at most 128 MiB of HBM per device.

```python
import math
import jax
import jax.numpy as jnp
import numpy as np
from jax import lax

NZ = 256
LABELS = 8
CLASSES = 16
ITERS = 2
NX = 64
NY = 64
N_AXIAL = 8
N_CIRC = 4


def draw_groups(key, part):
    own_key = jax.random.fold_in(key, 7)
    key_swap, key_other = jax.random.split(own_key)
    full_shape = (NX, NY, NZ)
    radial_pos = lax.broadcasted_iota(jnp.int32, full_shape, 2)
    layer_cells = NZ // LABELS
    base_label = radial_pos // layer_cells
    swapped = jax.random.randint(key_swap, full_shape, 0, 4, dtype=jnp.int32) == 0
    replacement = jax.random.randint(key_other, full_shape, 0, LABELS, dtype=jnp.int32)
    anchored = radial_pos % layer_cells == 0
    return jnp.where(jnp.logical_and(swapped, jnp.logical_not(anchored)), replacement, base_label).astype(jnp.int32)


def plant(entries, stream_key, low, top_value):
    index_at = [jax.random.randint(jax.random.fold_in(stream_key, axis), (), 0, length) for axis, length in enumerate(entries.shape)]
    widest = entries.shape.index(max(entries.shape))
    next_to = index_at[:widest] + [(index_at[widest] + 1) % entries.shape[widest]] + index_at[widest + 1:]
    return entries.at[tuple(index_at)].set(low).at[tuple(next_to)].set(top_value)


def level_of(key, dims, pieces, low, top_value):
    level = 1.0
    for axis_at, blocks in pieces:
        heights = jax.random.uniform(jax.random.fold_in(jax.random.fold_in(key, 6), axis_at), (blocks,), jnp.float32, low / len(pieces), top_value / len(pieces))
        level = level * jnp.repeat(jnp.exp(heights), dims[axis_at] // blocks).reshape((-1,) + (1,) * (len(dims) - 1 - axis_at))
    return level


def noise(stream_key, extent, scale, limit, pieces=(), kind=jnp.bfloat16):
    values = jax.random.normal(stream_key, extent, jnp.float32) * scale
    if len(pieces) > 0:
        values = level_of(stream_key, extent, pieces, -0.22, 0.18) * values
    return jnp.clip(values, min=-limit, max=limit).astype(kind)


def setup_inputs(seed: int = 0) -> dict:
    seeds = jax.random.split(jax.random.key(seed), 5)
    right_side = noise(seeds[0], (NX, NY, NZ), 1.0, 6.0, ((0, 8), (1, 4)), jnp.float32)
    stiffness = jnp.clip(jnp.exp(math.log(0.3) - 2.3025852 * jax.random.uniform(seeds[1], (NX, NY, NZ), jnp.float32) ** level_of(seeds[1], (NX, NY, NZ), ((0, 8), (1, 4)), -0.2, 0.2)), 0.03, 0.3)
    material = plant(jax.random.randint(seeds[2], (NX, NY, NZ), 0, CLASSES), jax.random.fold_in(seeds[2], 1), 0, CLASSES - 1).astype(jnp.int32)
    groups = draw_groups(jax.random.fold_in(seeds[4], 71), 0)
    return {"right_side": right_side, "stiffness": stiffness, "material": material, "groups": groups}


MASS_SHIFT = 0.02
PRECISE = lax.Precision.HIGHEST
HALF_STEPS = ((0, 0, 1), (0, 1, -1), (0, 1, 0), (0, 1, 1), (1, -1, -1), (1, -1, 0), (1, -1, 1), (1, 0, -1), (1, 0, 0), (1, 0, 1), (1, 1, -1), (1, 1, 0), (1, 1, 1))

def coefficient_table():
    rows_out = []
    for material_id in range(CLASSES):
        fiber_angle = math.pi * (material_id % 8) / 8.0
        if material_id < 8:
            fiber_dir = (math.cos(fiber_angle), math.sin(fiber_angle), 0.0)
            strength, anisotropy = (1.0, 6.0)
        else:
            fiber_dir = (0.6 * math.cos(fiber_angle), 0.6 * math.sin(fiber_angle), 0.8)
            strength, anisotropy = (0.35, 2.0)
        line_values = []
        for offset in HALF_STEPS:
            length_sq = float(offset[0] * offset[0] + offset[1] * offset[1] + offset[2] * offset[2])
            along_fiber = fiber_dir[0] * offset[0] + fiber_dir[1] * offset[1] + fiber_dir[2] * offset[2]
            line_values.append(strength * (0.15 + anisotropy * along_fiber * along_fiber / length_sq) / length_sq)
        rows_out.append(line_values)
    return np.array(rows_out, dtype=np.float32)

def shift_radial(values_in, amount):
    if amount == 0:
        return values_in
    blank_edge = jnp.zeros(values_in.shape[:-1] + (1,), values_in.dtype)
    if amount > 0:
        return jnp.concatenate([values_in[..., 1:], blank_edge], axis=-1)
    return jnp.concatenate([blank_edge, values_in[..., :-1]], axis=-1)

def neighbour(padded, move_axial, move_circ, move_radial):
    rows_axial = padded.shape[-3] - 2
    rows_circ = padded.shape[-2] - 2
    window = padded[..., 1 + move_axial:1 + move_axial + rows_axial, 1 + move_circ:1 + move_circ + rows_circ, :]
    return shift_radial(window, move_radial)

def pad_plane(values_in):
    wrapped = jnp.concatenate([values_in[:, -1:], values_in, values_in[:, :1]], axis=1)
    blank_rows = jnp.zeros((1,) + wrapped.shape[1:], wrapped.dtype)
    return jnp.concatenate([blank_rows, wrapped, blank_rows], axis=0)

def edge_weights(stiff_pad, class_pad):
    coef_table = jnp.asarray(coefficient_table())
    weights = []
    diagonal = None
    for position, offset in enumerate(HALF_STEPS):
        coefficient = stiff_pad * coef_table[:, position][class_pad]
        centre = coefficient[1:-1, 1:-1]
        forward_weight = 0.5 * (centre + neighbour(coefficient, offset[0], offset[1], offset[2]))
        backward_weight = 0.5 * (centre + neighbour(coefficient, -offset[0], -offset[1], -offset[2]))
        weights.append((forward_weight, backward_weight))
        pair_sum = forward_weight + backward_weight
        diagonal = pair_sum if diagonal is None else diagonal + pair_sum
    return (weights, MASS_SHIFT + diagonal)

def stencil_apply(padded, weights, diagonal):
    result = diagonal * padded[1:-1, 1:-1]
    for position, offset in enumerate(HALF_STEPS):
        forward_weight, backward_weight = weights[position]
        result = result - forward_weight * neighbour(padded, offset[0], offset[1], offset[2])
        result = result - backward_weight * neighbour(padded, -offset[0], -offset[1], -offset[2])
    return result

def block_factor(diagonal_blocks, upper_blocks):
    block_size = diagonal_blocks.shape[1]
    identity = jnp.eye(block_size, dtype=jnp.float32)

    def advance(carried, inputs):
        inverse_prev, upper_prev = carried
        diagonal_now, upper_now = inputs
        coupling = jnp.dot(inverse_prev, upper_prev, precision=PRECISE)
        schur_block = diagonal_now - jnp.dot(coupling.T, coupling, precision=PRECISE)
        factor_now = jnp.linalg.cholesky(schur_block)
        inverse_now = lax.linalg.triangular_solve(factor_now, identity, left_side=True, lower=True)
        return ((inverse_now, upper_now), (inverse_now, coupling))
    start = (identity, jnp.zeros((block_size, block_size), jnp.float32))
    unused, (inverses, couplings) = lax.scan(advance, start, (diagonal_blocks, upper_blocks))
    return (inverses, couplings)

def coarse_solve(inverses, couplings, coarse_rhs):
    cycle_count, block_size = (inverses.shape[0], inverses.shape[1])
    parts = coarse_rhs.reshape(cycle_count, block_size)

    def forward(previous, members):
        inverse_now, coupling, part_now = members
        target = part_now - jnp.dot(coupling.T, previous, precision=PRECISE)
        solved = jnp.dot(inverse_now, target, precision=PRECISE)
        return (solved, solved)
    unused, middle = lax.scan(forward, jnp.zeros((block_size,), jnp.float32), (inverses, couplings, parts))
    couplings_next = jnp.concatenate([couplings[1:], jnp.zeros((1, block_size, block_size), jnp.float32)], axis=0)

    def backward(solved_next, members):
        inverse_now, coupling_next, middle_now = members
        target = middle_now - jnp.dot(coupling_next, solved_next, precision=PRECISE)
        solved = jnp.dot(inverse_now.T, target, precision=PRECISE)
        return (solved, solved)
    unused_last, solution_parts = lax.scan(backward, jnp.zeros((block_size,), jnp.float32), (inverses, couplings_next, middle), reverse=True)
    return solution_parts.reshape(-1)

def reference(right_side, stiffness, material, groups):
    cells_axial, cells_circ, cells_radial = right_side.shape
    rows_axial = cells_axial // N_AXIAL
    rows_circ = cells_circ // N_CIRC
    coarse_count = LABELS * N_AXIAL * N_CIRC
    block_size = LABELS * N_CIRC
    weights, diagonal = edge_weights(pad_plane(stiffness), pad_plane(material))
    owner_axial = jnp.arange(cells_axial, dtype=jnp.int32) // rows_axial
    owner_circ = jnp.arange(cells_circ, dtype=jnp.int32) // rows_circ
    owner_id = owner_axial[:, None] * N_CIRC + owner_circ[None, :]
    coarse_index = (owner_id[:, :, None] * LABELS + groups).astype(jnp.int32)
    index_pad = pad_plane(coarse_index)
    inside_pad = pad_plane(jnp.ones_like(right_side))
    stencil_terms = [((0, 0, 0), diagonal)]
    for position, offset in enumerate(HALF_STEPS):
        forward_weight, backward_weight = weights[position]
        stencil_terms.append((offset, -forward_weight))
        stencil_terms.append(((-offset[0], -offset[1], -offset[2]), -backward_weight))
    coarse_flat = jnp.zeros((coarse_count * coarse_count,), jnp.float32)
    for offset, entry_value in stencil_terms:
        column_ids = neighbour(index_pad, offset[0], offset[1], offset[2]).astype(jnp.int32)
        inside = neighbour(inside_pad, offset[0], offset[1], offset[2])
        flat_ids = (coarse_index * coarse_count + column_ids).astype(jnp.int32)
        coarse_flat = coarse_flat.at[flat_ids.reshape(-1)].add((entry_value * inside).reshape(-1))
    coarse_four = coarse_flat.reshape(N_AXIAL, block_size, N_AXIAL, block_size)
    cycle_ids = jnp.arange(N_AXIAL, dtype=jnp.int32)
    diagonal_blocks = coarse_four[cycle_ids, :, cycle_ids, :]
    upper_blocks = jnp.concatenate([coarse_four[cycle_ids[:-1], :, cycle_ids[1:], :], jnp.zeros((1, block_size, block_size), jnp.float32)], axis=0)
    inverses, couplings = block_factor(diagonal_blocks, upper_blocks)

    def project(field):
        return jax.ops.segment_sum(field.reshape(-1), coarse_index.reshape(-1), num_segments=coarse_count)

    def spread(coarse_rhs):
        return coarse_solve(inverses, couplings, coarse_rhs)[coarse_index]

    def apply_global(field):
        return stencil_apply(pad_plane(field), weights, diagonal)
    solution = spread(project(right_side))
    residual = right_side - apply_global(solution)
    residual_image = apply_global(residual)
    norm_now = jnp.sum(residual * residual)
    direction = residual - spread(project(residual_image))
    for iteration in range(ITERS):
        direction_image = apply_global(direction)
        step_length = norm_now / jnp.sum(direction * direction_image)
        solution = solution + step_length * direction
        residual = residual - step_length * direction_image
        if iteration + 1 < ITERS:
            residual_image = apply_global(residual)
            norm_next = jnp.sum(residual * residual)
            shifted = spread(project(residual_image))
            beta_ratio = norm_next / norm_now
            direction = beta_ratio * direction + residual - shifted
            norm_now = norm_next
    return (solution, residual)
```

```python
import math

import jax
import jax.numpy as jnp
import numpy as np
from jax import lax
from jax.sharding import PartitionSpec as P

LABELS = 8
CLASSES = 16
ITERS = 2


MASS_SHIFT = 0.02
PRECISE = lax.Precision.HIGHEST
HALF_STEPS = (
    (0, 0, 1),
    (0, 1, -1),
    (0, 1, 0),
    (0, 1, 1),
    (1, -1, -1),
    (1, -1, 0),
    (1, -1, 1),
    (1, 0, -1),
    (1, 0, 0),
    (1, 0, 1),
    (1, 1, -1),
    (1, 1, 0),
    (1, 1, 1),
)


def with_halo(array, sides, width, wrap):
    for axis, dim in sides:
        peers, length = (lax.axis_size(axis), array.shape[dim])
        up = [(i, (i + 1) % peers) for i in range(peers if wrap else peers - 1)]
        down = [(j, i) for i, j in up]
        last = lax.slice_in_dim(array, length - width, length, axis=dim)
        first = lax.slice_in_dim(array, 0, width, axis=dim)
        before = lax.ppermute(last, axis, up)
        after = lax.ppermute(first, axis, down)
        array = jnp.concatenate([before, array, after], axis=dim)
    return array


def coefficient_table():
    rows_out = []
    for material_id in range(CLASSES):
        fiber_angle = math.pi * (material_id % 8) / 8.0
        if material_id < 8:
            fiber_dir = (math.cos(fiber_angle), math.sin(fiber_angle), 0.0)
            strength, anisotropy = (1.0, 6.0)
        else:
            fiber_dir = (0.6 * math.cos(fiber_angle), 0.6 * math.sin(fiber_angle), 0.8)
            strength, anisotropy = (0.35, 2.0)
        line_values = []
        for offset in HALF_STEPS:
            length_sq = float(offset[0] * offset[0] + offset[1] * offset[1] + offset[2] * offset[2])
            along_fiber = (
                fiber_dir[0] * offset[0] + fiber_dir[1] * offset[1] + fiber_dir[2] * offset[2]
            )
            line_values.append(
                strength * (0.15 + anisotropy * along_fiber * along_fiber / length_sq) / length_sq
            )
        rows_out.append(line_values)
    return np.array(rows_out, dtype=np.float32)


def shift_radial(values_in, amount):
    if amount == 0:
        return values_in
    blank_edge = jnp.zeros(values_in.shape[:-1] + (1,), values_in.dtype)
    if amount > 0:
        return jnp.concatenate([values_in[..., 1:], blank_edge], axis=-1)
    return jnp.concatenate([blank_edge, values_in[..., :-1]], axis=-1)


def neighbour(padded, move_axial, move_circ, move_radial):
    rows_axial = padded.shape[-3] - 2
    rows_circ = padded.shape[-2] - 2
    window = padded[
        ...,
        1 + move_axial : 1 + move_axial + rows_axial,
        1 + move_circ : 1 + move_circ + rows_circ,
        :,
    ]
    return shift_radial(window, move_radial)


def extend_field(field):
    widened = with_halo(field, (("circ", 1),), 1, True)
    return with_halo(widened, (("axial", 0),), 1, False)


def extend_labels(labels):
    widened = with_halo(labels, (("circ", 2),), 1, True)
    return with_halo(widened, (("axial", 1),), 1, False)


def class_onehot(labels, class_count):
    levels = jnp.arange(class_count, dtype=jnp.int32).reshape((class_count,) + (1,) * labels.ndim)
    return (labels[None] == levels).astype(jnp.float32)


def edge_weights(stiff_pad, class_pad):
    looked_up = jnp.einsum(
        "mxyr,mj->jxyr",
        class_onehot(class_pad, CLASSES),
        jnp.asarray(coefficient_table()),
        precision=PRECISE,
    )
    coefficient = stiff_pad[None] * looked_up
    weights = []
    diagonal = None
    for position, offset in enumerate(HALF_STEPS):
        centre = coefficient[position, 1:-1, 1:-1]
        forward_weight = 0.5 * (
            centre + neighbour(coefficient[position], offset[0], offset[1], offset[2])
        )
        backward_weight = 0.5 * (
            centre + neighbour(coefficient[position], -offset[0], -offset[1], -offset[2])
        )
        weights.append((forward_weight, backward_weight))
        pair_sum = forward_weight + backward_weight
        diagonal = pair_sum if diagonal is None else diagonal + pair_sum
    return (weights, MASS_SHIFT + diagonal)


def stencil_apply(padded, weights, diagonal):
    result = diagonal * padded[1:-1, 1:-1]
    for position, offset in enumerate(HALF_STEPS):
        forward_weight, backward_weight = weights[position]
        result = result - forward_weight * neighbour(padded, offset[0], offset[1], offset[2])
        result = result - backward_weight * neighbour(padded, -offset[0], -offset[1], -offset[2])
    return result


def coarse_panels(weights, diagonal, own_onehot, halo_onehot):
    stencil_terms = [((0, 0, 0), diagonal)]
    for position, offset in enumerate(HALF_STEPS):
        forward_weight, backward_weight = weights[position]
        stencil_terms.append((offset, -forward_weight))
        stencil_terms.append(((-offset[0], -offset[1], -offset[2]), -backward_weight))
    reached = None
    for offset, entry_value in stencil_terms:
        portion = shift_radial(own_onehot * entry_value[None], -offset[2])
        placed = jnp.pad(
            portion,
            ((0, 0), (1 + offset[0], 1 - offset[0]), (1 + offset[1], 1 - offset[1]), (0, 0)),
        )
        reached = placed if reached is None else reached + placed
    rows_axial = own_onehot.shape[1]
    rows_circ = own_onehot.shape[2]
    axial_parts = ((1, rows_axial + 1), (rows_axial + 1, rows_axial + 2))
    circ_parts = ((0, 1), (1, rows_circ + 1), (rows_circ + 1, rows_circ + 2))
    panel_rows = []
    for axial_start, axial_stop in axial_parts:
        panel_line = []
        for circ_start, circ_stop in circ_parts:
            panel_line.append(
                jnp.einsum(
                    "kxyr,lxyr->kl",
                    reached[:, axial_start:axial_stop, circ_start:circ_stop],
                    halo_onehot[:, axial_start:axial_stop, circ_start:circ_stop],
                    precision=PRECISE,
                )
            )
        panel_rows.append(jnp.stack(panel_line))
    return jnp.transpose(jnp.stack(panel_rows), (2, 0, 1, 3))


def cycle_blocks(panels):
    cycle_size = panels.shape[0]
    positions = jnp.arange(cycle_size, dtype=jnp.int32)
    shifts = jnp.stack(
        [
            ((positions[:, None] + offset) % cycle_size == positions[None, :]).astype(jnp.float32)
            for offset in (-1, 0, 1)
        ]
    )
    blocks = jnp.einsum("sjm,jkrsl->rjkml", shifts, panels, precision=PRECISE)
    return blocks.reshape(2, cycle_size * LABELS, cycle_size * LABELS)


def block_factor(diagonal_blocks, upper_blocks):
    block_size = diagonal_blocks.shape[1]
    identity = jnp.eye(block_size, dtype=jnp.float32)

    def advance(carried, inputs):
        inverse_prev, upper_prev = carried
        diagonal_now, upper_now = inputs
        coupling = jnp.dot(inverse_prev, upper_prev, precision=PRECISE)
        schur_block = diagonal_now - jnp.dot(coupling.T, coupling, precision=PRECISE)
        factor_now = jnp.linalg.cholesky(schur_block)
        inverse_now = lax.linalg.triangular_solve(factor_now, identity, left_side=True, lower=True)
        return ((inverse_now, upper_now), (inverse_now, coupling))

    start = (identity, jnp.zeros((block_size, block_size), jnp.float32))
    unused, (inverses, couplings) = lax.scan(advance, start, (diagonal_blocks, upper_blocks))
    return (inverses, couplings)


def coarse_solve(inverses, couplings, coarse_rhs):
    cycle_count, block_size = (inverses.shape[0], inverses.shape[1])
    parts = coarse_rhs.reshape(cycle_count, block_size, -1)

    def forward(previous, members):
        inverse_now, coupling, part_now = members
        target = part_now - jnp.dot(coupling.T, previous, precision=PRECISE)
        solved = jnp.dot(inverse_now, target, precision=PRECISE)
        return (solved, solved)

    unused, middle = lax.scan(
        forward, jnp.zeros((block_size, parts.shape[2]), jnp.float32), (inverses, couplings, parts)
    )
    couplings_next = jnp.concatenate(
        [couplings[1:], jnp.zeros((1, block_size, block_size), jnp.float32)], axis=0
    )

    def backward(solved_next, members):
        inverse_now, coupling_next, middle_now = members
        target = middle_now - jnp.dot(coupling_next, solved_next, precision=PRECISE)
        solved = jnp.dot(inverse_now.T, target, precision=PRECISE)
        return (solved, solved)

    unused_last, solution_parts = lax.scan(
        backward,
        jnp.zeros((block_size, parts.shape[2]), jnp.float32),
        (inverses, couplings_next, middle),
        reverse=True,
    )
    return solution_parts.reshape(cycle_count * block_size, -1)


def spread_coarse(coarse_values, halo_onehot, axial_index, circ_index, cycle_count, cycle_size):
    by_device = coarse_values.reshape(cycle_count, cycle_size, LABELS)
    grid_rows = []
    for move_axial in (-1, 0, 1):
        target = axial_index + move_axial
        present = jnp.logical_and(target >= 0, target < cycle_count)
        cycle_row = lax.dynamic_index_in_dim(
            by_device, jnp.clip(target, 0, cycle_count - 1), 0, keepdims=False
        )
        line_values = []
        for move_circ in (-1, 0, 1):
            beside = lax.dynamic_index_in_dim(
                cycle_row, (circ_index + move_circ) % cycle_size, 0, keepdims=False
            )
            line_values.append(jnp.where(present, beside, jnp.zeros_like(beside)))
        grid_rows.append(jnp.stack(line_values))
    regional = jnp.stack(grid_rows)
    rows_axial = halo_onehot.shape[1] - 2
    rows_circ = halo_onehot.shape[2] - 2
    regional = jnp.repeat(
        regional, np.array([1, rows_axial, 1]), axis=0, total_repeat_length=rows_axial + 2
    )
    regional = jnp.repeat(
        regional, np.array([1, rows_circ, 1]), axis=1, total_repeat_length=rows_circ + 2
    )
    return jnp.einsum("lxyr,xyl->xyr", halo_onehot, regional, precision=PRECISE)


def shards(right_side, stiffness, material, groups):
    cycle_count = lax.axis_size("axial")
    cycle_size = lax.axis_size("circ")
    axial_index = lax.axis_index("axial")
    circ_index = lax.axis_index("circ")
    labels_pad = extend_labels(jnp.stack([material, groups]))
    weights, diagonal = edge_weights(extend_field(stiffness), labels_pad[0])
    own_onehot = class_onehot(groups, LABELS)
    halo_onehot = class_onehot(labels_pad[1], LABELS)
    panels = coarse_panels(weights, diagonal, own_onehot, halo_onehot)
    cycle_panels = lax.all_gather(panels[None], "circ", axis=0, tiled=True)
    own_cycle = cycle_blocks(cycle_panels)
    all_cycles = lax.all_gather(own_cycle[None], "axial", axis=0, tiled=True)
    inverses, couplings = block_factor(all_cycles[:, 0], all_cycles[:, 1])

    def project(field):
        return jnp.einsum("kxyr,xyr->k", own_onehot, field, precision=PRECISE)

    size = cycle_count * cycle_size * LABELS
    coarse_inverse = coarse_solve(inverses, couplings, jnp.eye(size, dtype=jnp.float32))

    def coarse_gather(field, sums):
        own = jnp.concatenate([project(field)] + [value[None] for value in sums])
        gathered = lax.all_gather(own[None], ("axial", "circ"), axis=0, tiled=True)
        return (gathered[:, :LABELS].reshape(-1), jnp.sum(gathered[:, LABELS:], axis=0))

    def coarse_apply(coarse_rhs):
        return jnp.dot(coarse_inverse, coarse_rhs, precision=PRECISE)

    def spread_values(coarse_values):
        return spread_coarse(
            coarse_values, halo_onehot, axial_index, circ_index, cycle_count, cycle_size
        )

    def spread(coarse_rhs):
        return spread_values(coarse_apply(coarse_rhs))

    start_rhs, unused_sums = coarse_gather(right_side, ())
    start_pad = spread(start_rhs)
    solution = start_pad[1:-1, 1:-1]
    residual = right_side - stencil_apply(start_pad, weights, diagonal)
    direction = None
    for iteration in range(ITERS):
        residual_image = stencil_apply(extend_field(residual), weights, diagonal)
        sums = [jnp.sum(residual * residual), jnp.sum(residual * residual_image)]
        if direction is not None:
            sums.append(jnp.sum(residual * direction_image))
        coarse_rhs, totals = coarse_gather(residual_image, sums)
        coarse_values = coarse_apply(coarse_rhs)
        spread_pad = spread_values(coarse_values)
        curvature = totals[1] - jnp.sum(coarse_rhs * coarse_values)
        shifted = residual - spread_pad[1:-1, 1:-1]
        shifted_image = residual_image - stencil_apply(spread_pad, weights, diagonal)
        if direction is None:
            direction, direction_image = (shifted, shifted_image)
        else:
            ratio = totals[0] / norm_now
            curvature = ratio * ratio * curvature_now + 2.0 * ratio * totals[2] + curvature
            direction = ratio * direction + shifted
            direction_image = ratio * direction_image + shifted_image
        norm_now, curvature_now = (totals[0], curvature)
        step_length = norm_now / curvature
        solution = solution + step_length * direction
        residual = residual - step_length * direction_image
    return (solution, residual)


def solution(mesh):
    in_specs = (
        P("axial", "circ", None),
        P("axial", "circ", None),
        P("axial", "circ", None),
        P("axial", "circ", None),
    )
    out_specs = (P("axial", "circ", None), P("axial", "circ", None))
    return jax.shard_map(shards, mesh=mesh, in_specs=in_specs, out_specs=out_specs, check_vma=False)
```

```python
import functools
import math

import jax
import jax.numpy as jnp
from jax import lax
from jax.experimental import pallas as pl
from jax.experimental.pallas import tpu as pltpu
from jax.sharding import PartitionSpec as P

LABELS = 8
ITERS = 2
MASS_SHIFT = 0.02
PRECISE = lax.Precision.HIGHEST
MESH = pl.DeviceIdType.MESH
PAD = 8
LANES = 128
VMEM = pl.BlockSpec(memory_space=pltpu.VMEM)
HALF_STEPS = (
    (0, 0, 1),
    (0, 1, -1),
    (0, 1, 0),
    (0, 1, 1),
    (1, -1, -1),
    (1, -1, 0),
    (1, -1, 1),
    (1, 0, -1),
    (1, 0, 0),
    (1, 0, 1),
    (1, 1, -1),
    (1, 1, 0),
    (1, 1, 1),
)


SIDES = tuple((a, c) for a in (-1, 0, 1) for c in (-1, 0, 1) if (a, c) != (0, 0))
PANELS = ((0, 0), (0, 1), (1, -1), (1, 0), (1, 1))


def params(collective_id=None):
    if collective_id is None:
        return pltpu.CompilerParams(vmem_limit_bytes=56 * 1024 * 1024)
    return pltpu.CompilerParams(
        vmem_limit_bytes=56 * 1024 * 1024, collective_id=collective_id, has_side_effects=True
    )


def halo_kernel(count, *refs):
    fields = refs[:count]
    out, send_circ, send_axial, send_corner, recv_circ, recv_axial, recv_corner, send_sem, recv_sem = refs[count:]
    rows_axial, rows_circ, depth = fields[0].shape
    axials, circs = lax.axis_size("axial"), lax.axis_size("circ")
    axial, circ = lax.axis_index("axial"), lax.axis_index("circ")

    def inside(move):
        return jnp.logical_and(axial + move >= 0, axial + move < axials)

    def peer(side):
        return (axial + side[0], lax.rem(circ + side[1] + circs, circs))

    barrier = pltpu.get_barrier_semaphore()
    for side in SIDES:
        @pl.when(inside(side[0]))
        def _():
            pl.semaphore_signal(barrier, inc=1, device_id=peer(side), device_id_type=MESH)

    for f in range(count):
        value = fields[f][...].astype(jnp.float32)
        send_axial[0, f] = value[0]
        send_axial[1, f] = value[rows_axial - 1]
        for c in range(2):
            row = c * (rows_circ - 1)
            face = value[:, row, :]
            send_circ[c, f] = face
            for a in range(2):
                x = a * (rows_axial - 1)
                send_corner[2 * a + c, f] = face[x : x + 1]

    ends = jnp.where(axial == 0, 1, 0) + jnp.where(axial == axials - 1, 1, 0)
    pl.semaphore_wait(barrier, len(SIDES) - 3 * ends)

    def copy(side):
        a, c = (side[0] + 1) // 2, (side[1] + 1) // 2
        if side[0] == 0:
            source, target = send_circ.at[c], recv_circ.at[1 - c]
        elif side[1] == 0:
            source, target = send_axial.at[a], recv_axial.at[1 - a]
        else:
            source, target = send_corner.at[2 * a + c], recv_corner.at[3 - 2 * a - c]
        number = SIDES.index(side)
        return pltpu.make_async_remote_copy(
            src_ref=source,
            dst_ref=target,
            send_sem=send_sem.at[number],
            recv_sem=recv_sem.at[number],
            device_id=peer(side),
            device_id_type=MESH,
        )

    for side in SIDES:
        @pl.when(inside(side[0]))
        def _():
            copy(side).start()

    for f in range(count):
        for x in (0, rows_axial + 1):
            out[f, x] = jnp.zeros((rows_circ + 2 * PAD, depth), jnp.float32)
        blank = jnp.zeros((rows_axial, PAD, depth), jnp.float32)
        out[f, 1 : rows_axial + 1, 0:PAD, :] = blank
        out[f, 1 : rows_axial + 1, PAD + rows_circ :, :] = blank
        out[f, 1 : rows_axial + 1, PAD : PAD + rows_circ, :] = fields[f][...].astype(jnp.float32)

    edge = (PAD - 1, PAD + rows_circ)
    for side in SIDES:
        a, c = (1 - side[0]) // 2, (1 - side[1]) // 2
        x = a * (rows_axial + 1)

        @pl.when(inside(-side[0]))
        def _():
            copy(side).wait_recv()
            for f in range(count):
                if side[0] == 0:
                    for row in range(rows_axial):
                        out[f, row + 1, edge[c] : edge[c] + 1, :] = recv_circ[c, f, row : row + 1, :]
                elif side[1] == 0:
                    out[f, x, PAD : PAD + rows_circ, :] = recv_axial[a, f]
                else:
                    out[f, x, edge[c] : edge[c] + 1, :] = recv_corner[2 * a + c, f]

    for side in SIDES:
        @pl.when(inside(side[0]))
        def _():
            copy(side).wait_send()


def halo(fields, collective_id):
    count = len(fields)
    rows_axial, rows_circ, depth = fields[0].shape
    buffers = [
        pltpu.VMEM((2, count, rows_axial, depth), jnp.float32),
        pltpu.VMEM((2, count, rows_circ, depth), jnp.float32),
        pltpu.VMEM((4, count, 1, depth), jnp.float32),
    ]
    return pl.pallas_call(
        functools.partial(halo_kernel, count),
        out_shape=jax.ShapeDtypeStruct(
            (count, rows_axial + 2, rows_circ + 2 * PAD, depth), jnp.float32
        ),
        in_specs=[VMEM] * count,
        out_specs=VMEM,
        scratch_shapes=buffers
        + buffers
        + [pltpu.SemaphoreType.DMA((len(SIDES),)), pltpu.SemaphoreType.DMA((len(SIDES),))],
        compiler_params=params(collective_id),
        name="halo",
    )(*fields)


def gather_kernel(own, out, send_sem, recv_sem):
    axials, circs = lax.axis_size("axial"), lax.axis_size("circ")
    devices = axials * circs
    me = lax.axis_index("axial") * circs + lax.axis_index("circ")

    def place(number):
        return (number // circs, lax.rem(number, circs))

    barrier = pltpu.get_barrier_semaphore()

    def greet(step, carry):
        pl.semaphore_signal(
            barrier, inc=1, device_id=place(lax.rem(me + step, devices)), device_id_type=MESH
        )
        return carry

    lax.fori_loop(1, devices, greet, 0)
    pl.semaphore_wait(barrier, devices - 1)

    def copy(step, slot):
        return pltpu.make_async_remote_copy(
            src_ref=own,
            dst_ref=out.at[slot],
            send_sem=send_sem.at[step],
            recv_sem=recv_sem.at[step],
            device_id=place(lax.rem(me + step, devices)),
            device_id_type=MESH,
        )

    def send(step, carry):
        copy(step, me).start()
        return carry

    lax.fori_loop(1, devices, send, 0)
    out[me] = own[...]

    def finish(step, carry):
        copy(step, lax.rem(me - step + devices, devices)).wait_recv()
        copy(step, me).wait_send()
        return carry

    lax.fori_loop(1, devices, finish, 0)


def gather(own, collective_id):
    devices = lax.axis_size("axial") * lax.axis_size("circ")
    out = pl.pallas_call(
        gather_kernel,
        out_shape=jax.ShapeDtypeStruct((devices,) + own.shape, jnp.float32),
        in_specs=[VMEM],
        out_specs=VMEM,
        scratch_shapes=[
            pltpu.SemaphoreType.DMA((devices,)),
            pltpu.SemaphoreType.DMA((devices,)),
        ],
        compiler_params=params(collective_id),
        name="gather",
    )(own)
    return out.reshape(devices * LABELS, LANES)


def shifted(window, move):
    if move == 0:
        return window
    depth = window.shape[-1]
    lane = lax.broadcasted_iota(jnp.int32, window.shape, window.ndim - 1)
    rolled = pltpu.roll(window, (depth - move) % depth, window.ndim - 1)
    return jnp.where(lane == (depth - 1 if move > 0 else 0), 0.0, rolled)


def window_of(ref, x, rows_circ, offset):
    return ref[x + 1 + offset[0], PAD + offset[1] : PAD + offset[1] + rows_circ, :]


def opposite(offset):
    return (-offset[0], -offset[1], -offset[2])


def terms():
    listed = []
    for position, offset in enumerate(HALF_STEPS):
        listed.append((position, offset))
        listed.append((len(HALF_STEPS) + position, opposite(offset)))
    return sorted(listed, key=lambda term: term[1])


def in_sums(sums):
    lane = lax.broadcasted_iota(jnp.int32, (LABELS, LANES), 1)
    tile = jnp.zeros((LABELS, LANES), jnp.float32)
    for position, value in sums:
        tile = tile + jnp.where(lane == position, value, 0.0)
    return tile


def label_sums(groups_ref, field_of, rows_axial, rows_circ, depth):
    def plane(x, sums):
        labels = window_of(groups_ref, x, rows_circ, (0, 0))
        value = field_of(x)
        return tuple(
            total + jnp.where(labels == float(label), value, 0.0)
            for label, total in enumerate(sums)
        )

    blank = jnp.zeros((rows_circ, depth), jnp.float32)
    sums = lax.fori_loop(0, rows_axial, plane, (blank,) * LABELS)
    rows = [jnp.sum(total, axis=0, keepdims=True) for total in sums]
    return jnp.sum(jnp.concatenate(rows, axis=0), axis=1, keepdims=True)


def weights_kernel(ext, right, weights, panel, stiff, seen, total):
    rows_axial, rows_circ, depth = right.shape
    groups = ext.at[2]
    half = len(HALF_STEPS)

    def stiffness_plane(x, carry):
        scale = ext[0, x]
        material = ext[1, x]
        upper = material >= 8.0
        angle = material - jnp.where(upper, 8.0, 0.0)
        first = jnp.full_like(scale, 1.0)
        second = jnp.zeros_like(scale)
        for turn in range(1, 8):
            first = jnp.where(angle == float(turn), math.cos(math.pi * turn / 8.0), first)
            second = jnp.where(angle == float(turn), math.sin(math.pi * turn / 8.0), second)
        shrink = jnp.where(upper, 0.6, 1.0)
        first, second = first * shrink, second * shrink
        third = jnp.where(upper, 0.8, 0.0)
        flat = scale * jnp.where(upper, 0.35 * 0.15, 0.15)
        along = scale * jnp.where(upper, 0.35 * 2.0, 6.0)
        for position, offset in enumerate(HALF_STEPS):
            length = float(sum(part * part for part in offset))
            dot = None
            for part, line in zip(offset, (first, second, third)):
                if part != 0:
                    line = line if part > 0 else -line
                    dot = line if dot is None else dot + line
            stiff[position, x] = flat * (1.0 / length) + along * (dot * dot) * (1.0 / (length * length))
        return carry

    lax.fori_loop(0, rows_axial + 2, stiffness_plane, 0)

    def weight_plane(x, carry):
        diagonal = None
        for position, offset in enumerate(HALF_STEPS):
            field = stiff.at[position]
            centre = window_of(field, x, rows_circ, (0, 0))
            ahead = 0.5 * (centre + shifted(window_of(field, x, rows_circ, offset), offset[2]))
            back = opposite(offset)
            behind = 0.5 * (centre + shifted(window_of(field, x, rows_circ, back), back[2]))
            weights[position, x] = ahead
            weights[half + position, x] = behind
            pair = ahead + behind
            diagonal = pair if diagonal is None else diagonal + pair
        weights[2 * half, x] = MASS_SHIFT + diagonal
        return carry

    lax.fori_loop(0, rows_axial, weight_plane, 0)

    row = lax.broadcasted_iota(jnp.int32, (rows_circ, depth), 0)
    listed = terms()
    total[...] = jnp.zeros_like(total)

    def own_labels(x):
        labels = window_of(groups, x, rows_circ, (0, 0))
        return jnp.concatenate(
            [jnp.where(labels == float(label), 1.0, 0.0) for label in range(LABELS)], axis=0
        )

    def seen_labels(offset, x):
        labels = window_of(groups, x, rows_circ, offset)
        if offset[2] == 0:
            return labels
        lane = lax.broadcasted_iota(jnp.int32, labels.shape, 1)
        rolled = pltpu.roll(labels, (depth - offset[2]) % depth, 1)
        return jnp.where(lane == (depth - 1 if offset[2] > 0 else 0), -1.0, rolled)

    def add_panel(slot, x, parts):
        found = jnp.concatenate(parts, axis=0)
        total[slot] += lax.dot_general(
            own_labels(x),
            found,
            (((1,), (1,)), ((), ())),
            precision=PRECISE,
            preferred_element_type=jnp.float32,
        )

    def panel_plane(x, carry):
        for number, (position, offset) in enumerate(listed):
            labels = seen_labels(offset, x)
            leaves = None
            if offset[1] != 0:
                leaves = row == (rows_circ - 1 if offset[1] > 0 else 0)
            if offset[0] != 0:
                edge = x == (rows_axial - 1 if offset[0] > 0 else 0)
                labels = jnp.where(edge, -1.0, labels)
            seen[number] = labels if leaves is None else jnp.where(leaves, -1.0, labels)
        parts, beside = [], []
        centre = window_of(groups, x, rows_circ, (0, 0))
        for label in range(LABELS):
            found = jnp.where(centre == float(label), weights[2 * half, x], 0.0)
            for number, (position, offset) in enumerate(listed):
                found = found - jnp.where(seen[number] == float(label), weights[position, x], 0.0)
            parts.append(found)
        add_panel(0, x, parts)
        for number, (position, offset) in enumerate(listed):
            if offset[1] > 0:
                labels = seen_labels(offset, x)
                if offset[0] != 0:
                    edge = x == (rows_axial - 1 if offset[0] > 0 else 0)
                    labels = jnp.where(edge, -1.0, labels)
                seen[number] = jnp.where(row == rows_circ - 1, labels, -1.0)
        for label in range(LABELS):
            found = jnp.zeros((rows_circ, depth), jnp.float32)
            for number, (position, offset) in enumerate(listed):
                if offset[1] > 0:
                    found = found - jnp.where(
                        seen[number] == float(label), weights[position, x], 0.0
                    )
            beside.append(found)
        add_panel(1, x, beside)
        return carry

    lax.fori_loop(0, rows_axial, panel_plane, 0)

    last = rows_axial - 1
    for slot in range(2, len(PANELS)):
        move = PANELS[slot][1]
        chosen = []
        for position, offset in listed:
            if offset[0] > 0 and (offset[1] == move or move == 0):
                labels = seen_labels(offset, last)
                if offset[1] != 0:
                    leaves = row == (rows_circ - 1 if offset[1] > 0 else 0)
                    labels = jnp.where(leaves == (move != 0), labels, -1.0)
                chosen.append((position, labels))
        parts = []
        for label in range(LABELS):
            found = jnp.zeros((rows_circ, depth), jnp.float32)
            for position, labels in chosen:
                found = found - jnp.where(labels == float(label), weights[position, last], 0.0)
            parts.append(found)
        add_panel(slot, last, parts)

    size = LABELS * rows_circ
    line = lax.broadcasted_iota(jnp.int32, (size, size), 0)
    column = lax.broadcasted_iota(jnp.int32, (size, size), 1)
    same = lax.rem(line, rows_circ) == lax.rem(column, rows_circ)
    tile_row = lax.broadcasted_iota(jnp.int32, (LABELS, size), 0)
    tile_column = lax.broadcasted_iota(jnp.int32, (LABELS, size), 1)
    collect = jnp.where(tile_column // rows_circ == tile_row, 1.0, 0.0)
    spot_row = lax.broadcasted_iota(jnp.int32, (size, LANES), 0)
    spot_column = lax.broadcasted_iota(jnp.int32, (size, LANES), 1)
    result = jnp.zeros((LABELS, LANES), jnp.float32)
    for slot in range(len(PANELS)):
        lines = jnp.dot(collect, jnp.where(same, total[slot], 0.0), precision=PRECISE)
        spots = jnp.where(spot_row // rows_circ + slot * LABELS == spot_column, 1.0, 0.0)
        result = result + jnp.dot(lines, spots, precision=PRECISE)
    own = label_sums(groups, lambda x: right[x], rows_axial, rows_circ, depth)
    panel[...] = result + in_sums([(len(PANELS) * LABELS, own)])


def inverse_of(matrix):
    size = matrix.shape[0]
    line = lax.broadcasted_iota(jnp.int32, (size, size), 0)
    column = lax.broadcasted_iota(jnp.int32, (size, size), 1)
    for step in range(size):
        pivot = 1.0 / matrix[step : step + 1, step : step + 1]
        across = matrix[step : step + 1, :] * pivot
        down = matrix[:, step : step + 1]
        in_line, in_column = line == step, column == step
        rest = jnp.where(in_column, 0.0, matrix) - down * jnp.where(in_column[0:1], pivot, across)
        matrix = jnp.where(in_line, jnp.where(in_column, pivot, across), rest)
    return matrix


def coarse_kernel(cycles, gathered, inverse, diagonals, uppers, held, linked, partial):
    size = gathered.shape[0] // cycles
    whole = gathered.shape[0]
    circs = size // LABELS
    line = lax.broadcasted_iota(jnp.int32, (size, size), 0) // LABELS
    column = lax.broadcasted_iota(jnp.int32, (size, size), 1) // LABELS
    spread_row = lax.broadcasted_iota(jnp.int32, (LANES, size), 0)
    spread_column = lax.rem(lax.broadcasted_iota(jnp.int32, (LANES, size), 1), LABELS)

    def dot(left, right):
        return jnp.dot(left, right, precision=PRECISE, preferred_element_type=jnp.float32)

    def block(s, slot):
        tiles = jnp.where(spread_row == spread_column + slot * LABELS, 1.0, 0.0)
        placed = dot(gathered[pl.ds(s * size, size), :], tiles)
        return jnp.where(lax.rem(line + PANELS[slot][1] + circs, circs) == column, placed, 0.0)

    def assemble(s, carry):
        beside = block(s, 1)
        diagonals[s] = block(s, 0) + beside + beside.T
        uppers[s] = block(s, 2) + block(s, 3) + block(s, 4)
        return carry

    lax.fori_loop(0, cycles, assemble, 0)
    unit_line = lax.broadcasted_iota(jnp.int32, (size, whole), 0)
    unit_column = lax.broadcasted_iota(jnp.int32, (size, whole), 1)

    def unit(s):
        return jnp.where(unit_line + s * size == unit_column, 1.0, 0.0)

    def eliminate(s, s_next, upper):
        inverted = inverse_of(diagonals[s])
        link = dot(inverted, upper)
        held[s] = inverted
        linked[s] = link
        across = upper.T
        diagonals[s_next] = diagonals[s_next] - dot(across, link)
        partial[s_next] = partial[s_next] - dot(link.T, partial[s])

    def start(s, carry):
        partial[s] = unit(s)
        return carry

    lax.fori_loop(0, cycles, start, 0)
    middle = cycles // 2

    def from_both_ends(step, carry):
        low, high = step, cycles - 1 - step
        upper_low, upper_high = uppers[low], uppers[high - 1].T
        inverted_low, inverted_high = inverse_pair(diagonals[low], diagonals[high])
        for s, s_next, upper, inverted in (
            (low, low + 1, upper_low, inverted_low),
            (high, high - 1, upper_high, inverted_high),
        ):
            link = dot(inverted, upper)
            held[s] = inverted
            linked[s] = link
            diagonals[s_next] = diagonals[s_next] - dot(upper.T, link)
            partial[s_next] = partial[s_next] - dot(link.T, partial[s])
        return carry

    lax.fori_loop(0, middle - 1, from_both_ends, 0)
    eliminate(middle - 1, middle, uppers[middle - 1])
    rows = pl.ds(middle * size, size)
    inverse[rows, :] = dot(inverse_of(diagonals[middle]), partial[middle])

    def put(s, s_next):
        ahead = inverse[pl.ds(s_next * size, size), :]
        inverse[pl.ds(s * size, size), :] = dot(held[s], partial[s]) - dot(linked[s], ahead)

    put(middle - 1, middle)

    def back(step, carry):
        put(middle - 2 - step, middle - 1 - step)
        put(middle + 1 + step, middle + step)
        return carry

    lax.fori_loop(0, middle - 1, back, 0)


def inverse_pair(first, second):
    return inverse_of(first), inverse_of(second)


def coarse_inverse(gathered):
    cycles, circs = lax.axis_size("axial"), lax.axis_size("circ")
    size, whole = circs * LABELS, gathered.shape[0]
    square = pltpu.VMEM((cycles, size, size), jnp.float32)
    return pl.pallas_call(
        functools.partial(coarse_kernel, cycles),
        out_shape=jax.ShapeDtypeStruct((whole, whole), jnp.float32),
        in_specs=[VMEM],
        out_specs=VMEM,
        scratch_shapes=[square] * 4 + [pltpu.VMEM((cycles, size, whole), jnp.float32)],
        compiler_params=params(),
        name="coarse_inverse",
    )(gathered)


def apply_plane(ext, weights, x, rows_circ):
    centre = 2 * len(HALF_STEPS)
    result = weights[centre, x] * window_of(ext, x, rows_circ, (0, 0))
    for position, offset in terms():
        value = shifted(window_of(ext, x, rows_circ, offset), offset[2])
        result = result - weights[position, x] * value
    return result


def spread_into(spread, values, column, groups):
    planes, rows, depth = spread.shape
    axials, circs = lax.axis_size("axial"), lax.axis_size("circ")
    axial, circ = lax.axis_index("axial"), lax.axis_index("circ")
    row = lax.broadcasted_iota(jnp.int32, (rows, depth), 0)

    def tile(a, c):
        at = axial + a
        present = jnp.logical_and(at >= 0, at < axials)
        at = jnp.minimum(jnp.maximum(at, 0), axials - 1)
        number = at * circs + lax.rem(circ + c + circs, circs)
        part = values[pl.ds(pl.multiple_of(number * LABELS, LABELS), LABELS), column : column + 1]
        return jnp.where(present, jnp.broadcast_to(part, (LABELS, depth)), 0.0)

    def fill(x, sides):
        labels = groups[x]
        value = jnp.zeros((rows, depth), jnp.float32)
        for label in range(LABELS):
            before, here, after = [side[label : label + 1, :] for side in sides]
            chosen = jnp.where(row < PAD, before, jnp.where(row < rows - PAD, here, after))
            value = jnp.where(labels == float(label), chosen, value)
        spread[x] = value

    fill(0, [tile(-1, c) for c in (-1, 0, 1)])
    fill(planes - 1, [tile(1, c) for c in (-1, 0, 1)])
    sides = [tile(0, c) for c in (-1, 0, 1)]

    def inner(x, carry):
        fill(x, sides)
        return carry

    lax.fori_loop(1, planes - 1, inner, 0)


def start_kernel(inverse, gathered, ext, weights, right, solution, residual, values, spread):
    rows_axial, rows_circ, depth = right.shape
    values[...] = jnp.dot(inverse[...], gathered[...], precision=PRECISE)
    spread_into(spread, values, len(PANELS) * LABELS, ext.at[2])

    def plane(x, carry):
        solution[x] = window_of(spread, x, rows_circ, (0, 0))
        residual[x] = right[x] - apply_plane(spread, weights, x, rows_circ)
        return carry

    lax.fori_loop(0, rows_axial, plane, 0)


def image_kernel(later, *refs):
    if later:
        residual_ext, ext, weights, direction_image, image, sums = refs
    else:
        residual_ext, ext, weights, image, sums = refs
    rows_axial, rows_circ, depth = image.shape
    field = residual_ext.at[0]

    def plane(x, totals):
        value = apply_plane(field, weights, x, rows_circ)
        image[x] = value
        residual = window_of(field, x, rows_circ, (0, 0))
        factors = [residual, value] + ([direction_image[x]] if later else [])
        return tuple(total + residual * factor for total, factor in zip(totals, factors))

    blank = jnp.zeros((rows_circ, depth), jnp.float32)
    totals = lax.fori_loop(0, rows_axial, plane, (blank,) * (3 if later else 2))
    found = [(0, label_sums(ext.at[2], lambda x: image[x], rows_axial, rows_circ, depth))]
    line = lax.broadcasted_iota(jnp.int32, (LABELS, LANES), 0)
    for position, total in enumerate(totals):
        whole = jnp.sum(jnp.sum(total, axis=0, keepdims=True), axis=1, keepdims=True)
        found.append((position + 1, jnp.where(line == 0, whole, 0.0)))
    sums[...] = in_sums(found)


def update_kernel(later, final, *refs):
    inverse, gathered, ext, weights, solution, residual, image = refs[:7]
    refs = refs[7:]
    if later:
        direction, direction_image, scalars = refs[:3]
        refs = refs[3:]
    solution_out, residual_out = refs[:2]
    refs = refs[2:]
    if not final:
        direction_out, direction_image_out, scalars_out = refs[:3]
        refs = refs[3:]
    values, spread = refs
    rows_axial, rows_circ, depth = solution.shape
    values[...] = jnp.dot(inverse[...], gathered[...], precision=PRECISE)
    spread_into(spread, values, 0, ext.at[2])
    totals = jnp.sum(gathered[...], axis=0, keepdims=True)
    norm = totals[:, 1:2]
    overlap = jnp.sum(gathered[...] * values[...], axis=0, keepdims=True)[:, 0:1]
    curvature = totals[:, 2:3] - overlap
    if later:
        ratio = norm / scalars[0:1, 0:1]
        curvature = ratio * ratio * scalars[0:1, 1:2] + 2.0 * ratio * totals[:, 3:4] + curvature
    step = norm / curvature

    def plane(x, carry):
        now = residual[x]
        along = now - window_of(spread, x, rows_circ, (0, 0))
        along_image = image[x] - apply_plane(spread, weights, x, rows_circ)
        if later:
            along = along + ratio * direction[x]
            along_image = along_image + ratio * direction_image[x]
        solution_out[x] = solution[x] + step * along
        residual_out[x] = now - step * along_image
        if not final:
            direction_out[x] = along
            direction_image_out[x] = along_image
        return carry

    lax.fori_loop(0, rows_axial, plane, 0)
    if not final:
        scalars_out[...] = in_sums([(0, norm), (1, curvature)])


def call(kernel, outs, scratch, args, name):
    return pl.pallas_call(
        kernel,
        out_shape=[jax.ShapeDtypeStruct(shape, jnp.float32) for shape in outs],
        in_specs=[VMEM] * len(args),
        out_specs=[VMEM] * len(outs),
        scratch_shapes=[pltpu.VMEM(shape, jnp.float32) for shape in scratch],
        compiler_params=params(),
        name=name,
    )(*args)


def shards(right_side, stiffness, material, groups):
    block = right_side.shape
    rows_axial, rows_circ, depth = block
    padded = (rows_axial + 2, rows_circ + 2 * PAD, depth)
    count = 2 * len(HALF_STEPS) + 1
    tile = (LABELS, LANES)
    size = LABELS * rows_circ
    ext = halo([stiffness, material, groups], 0)
    weights, panel = call(
        weights_kernel,
        [(count,) + block, tile],
        [(len(HALF_STEPS),) + padded, (count, rows_circ, depth), (len(PANELS), size, size)],
        [ext, right_side],
        "weights",
    )
    gathered = gather(panel, 1)
    inverse = coarse_inverse(gathered)
    work = [gathered.shape, padded]
    solution, residual = call(
        start_kernel, [block, block], work, [inverse, gathered, ext, weights, right_side], "start"
    )
    carried = []
    for iteration in range(ITERS):
        later, final = iteration > 0, iteration + 1 == ITERS
        residual_ext = halo([residual], 2 + 2 * iteration)
        image, sums = call(
            functools.partial(image_kernel, later),
            [block, tile],
            [],
            [residual_ext, ext, weights] + carried[1:2],
            "image",
        )
        gathered = gather(sums, 3 + 2 * iteration)
        solution, residual, *carried = call(
            functools.partial(update_kernel, later, final),
            [block, block] + ([] if final else [block, block, tile]),
            work,
            [inverse, gathered, ext, weights, solution, residual, image] + carried,
            "update",
        )
    return (solution, residual)


def solution(mesh):
    in_specs = (
        P("axial", "circ", None),
        P("axial", "circ", None),
        P("axial", "circ", None),
        P("axial", "circ", None),
    )
    out_specs = (P("axial", "circ", None), P("axial", "circ", None))
    return jax.shard_map(shards, mesh=mesh, in_specs=in_specs, out_specs=out_specs, check_vma=False)
```

```python
import functools
import math

import jax
import jax.numpy as jnp
from jax import lax
from jax.experimental import pallas as pl
from jax.experimental.pallas import tpu as pltpu
from jax.sharding import PartitionSpec as P

LABELS = 8
ITERS = 2
MASS_SHIFT = 0.02
PRECISE = lax.Precision.HIGHEST
MESH = pl.DeviceIdType.MESH
PAD = 8
LANES = 128
VMEM = pl.BlockSpec(memory_space=pltpu.VMEM)
HALF_STEPS = (
    (0, 0, 1),
    (0, 1, -1),
    (0, 1, 0),
    (0, 1, 1),
    (1, -1, -1),
    (1, -1, 0),
    (1, -1, 1),
    (1, 0, -1),
    (1, 0, 0),
    (1, 0, 1),
    (1, 1, -1),
    (1, 1, 0),
    (1, 1, 1),
)


SIDES = tuple((a, c) for a in (-1, 0, 1) for c in (-1, 0, 1) if (a, c) != (0, 0))
PANELS = ((0, 0), (0, 1), (1, -1), (1, 0), (1, 1))


def params(collective_id=None):
    if collective_id is None:
        return pltpu.CompilerParams(vmem_limit_bytes=56 * 1024 * 1024)
    return pltpu.CompilerParams(
        vmem_limit_bytes=56 * 1024 * 1024, collective_id=collective_id, has_side_effects=True
    )


def halo_kernel(count, *refs):
    fields = refs[:count]
    out, send_circ, send_axial, send_corner, recv_circ, recv_axial, recv_corner, send_sem, recv_sem = refs[count:]
    rows_axial, rows_circ, depth = fields[0].shape
    axials, circs = lax.axis_size("axial"), lax.axis_size("circ")
    axial, circ = lax.axis_index("axial"), lax.axis_index("circ")

    def inside(move):
        return jnp.logical_and(axial + move >= 0, axial + move < axials)

    def peer(side):
        return (axial + side[0], lax.rem(circ + side[1] + circs, circs))

    barrier = pltpu.get_barrier_semaphore()
    for side in SIDES:
        @pl.when(inside(side[0]))
        def _():
            pl.semaphore_signal(barrier, inc=1, device_id=peer(side), device_id_type=MESH)

    for f in range(count):
        value = fields[f][...].astype(jnp.float32)
        send_axial[0, f] = value[0]
        send_axial[1, f] = value[rows_axial - 1]
        for c in range(2):
            row = c * (rows_circ - 1)
            face = value[:, row, :]
            send_circ[c, f] = face
            for a in range(2):
                x = a * (rows_axial - 1)
                send_corner[2 * a + c, f] = face[x : x + 1]

    ends = jnp.where(axial == 0, 1, 0) + jnp.where(axial == axials - 1, 1, 0)
    pl.semaphore_wait(barrier, len(SIDES) - 3 * ends)

    def copy(side):
        a, c = (side[0] + 1) // 2, (side[1] + 1) // 2
        if side[0] == 0:
            source, target = send_circ.at[c], recv_circ.at[1 - c]
        elif side[1] == 0:
            source, target = send_axial.at[a], recv_axial.at[1 - a]
        else:
            source, target = send_corner.at[2 * a + c], recv_corner.at[3 - 2 * a - c]
        number = SIDES.index(side)
        return pltpu.make_async_remote_copy(
            src_ref=source,
            dst_ref=target,
            send_sem=send_sem.at[number],
            recv_sem=recv_sem.at[number],
            device_id=peer(side),
            device_id_type=MESH,
        )

    for side in SIDES:
        @pl.when(inside(side[0]))
        def _():
            copy(side).start()

    for f in range(count):
        for x in (0, rows_axial + 1):
            out[f, x] = jnp.zeros((rows_circ + 2 * PAD, depth), jnp.float32)
        blank = jnp.zeros((rows_axial, PAD, depth), jnp.float32)
        out[f, 1 : rows_axial + 1, 0:PAD, :] = blank
        out[f, 1 : rows_axial + 1, PAD + rows_circ :, :] = blank
        out[f, 1 : rows_axial + 1, PAD : PAD + rows_circ, :] = fields[f][...].astype(jnp.float32)

    edge = (PAD - 1, PAD + rows_circ)
    for side in SIDES:
        a, c = (1 - side[0]) // 2, (1 - side[1]) // 2
        x = a * (rows_axial + 1)

        @pl.when(inside(-side[0]))
        def _():
            copy(side).wait_recv()
            for f in range(count):
                if side[0] == 0:
                    for row in range(rows_axial):
                        out[f, row + 1, edge[c] : edge[c] + 1, :] = recv_circ[c, f, row : row + 1, :]
                elif side[1] == 0:
                    out[f, x, PAD : PAD + rows_circ, :] = recv_axial[a, f]
                else:
                    out[f, x, edge[c] : edge[c] + 1, :] = recv_corner[2 * a + c, f]

    for side in SIDES:
        @pl.when(inside(side[0]))
        def _():
            copy(side).wait_send()


def halo(fields, collective_id):
    count = len(fields)
    rows_axial, rows_circ, depth = fields[0].shape
    buffers = [
        pltpu.VMEM((2, count, rows_axial, depth), jnp.float32),
        pltpu.VMEM((2, count, rows_circ, depth), jnp.float32),
        pltpu.VMEM((4, count, 1, depth), jnp.float32),
    ]
    return pl.pallas_call(
        functools.partial(halo_kernel, count),
        out_shape=jax.ShapeDtypeStruct(
            (count, rows_axial + 2, rows_circ + 2 * PAD, depth), jnp.float32
        ),
        in_specs=[VMEM] * count,
        out_specs=VMEM,
        scratch_shapes=buffers
        + buffers
        + [pltpu.SemaphoreType.DMA((len(SIDES),)), pltpu.SemaphoreType.DMA((len(SIDES),))],
        compiler_params=params(collective_id),
        name="halo",
    )(*fields)


def gather_kernel(own, out, send_sem, recv_sem):
    axials, circs = lax.axis_size("axial"), lax.axis_size("circ")
    axial, circ = lax.axis_index("axial"), lax.axis_index("circ")
    me = axial * circs + circ
    greet(axial, circ, axials, circs)
    exchange(own, out, send_sem, recv_sem)


def greet(axial, circ, axials, circs):
    barrier = pltpu.get_barrier_semaphore()
    for step in range(1, circs):
        pl.semaphore_signal(
            barrier, inc=1, device_id=(axial, lax.rem(circ + step, circs)), device_id_type=MESH
        )
    for step in range(1, axials):
        pl.semaphore_signal(
            barrier, inc=1, device_id=(lax.rem(axial + step, axials), circ), device_id_type=MESH
        )
    pl.semaphore_wait(barrier, axials + circs - 2)


def exchange(own, out, send_sem, recv_sem):
    axials, circs = lax.axis_size("axial"), lax.axis_size("circ")
    axial, circ = lax.axis_index("axial"), lax.axis_index("circ")
    me = axial * circs + circ

    def beside(step, slot):
        return pltpu.make_async_remote_copy(
            src_ref=own,
            dst_ref=out.at[slot],
            send_sem=send_sem.at[step],
            recv_sem=recv_sem.at[step],
            device_id=(axial, lax.rem(circ + step, circs)),
            device_id_type=MESH,
        )

    def along(step, cycle):
        part = out.at[pl.ds(cycle * circs, circs)]
        return pltpu.make_async_remote_copy(
            src_ref=part,
            dst_ref=part,
            send_sem=send_sem.at[circs + step],
            recv_sem=recv_sem.at[circs + step],
            device_id=(lax.rem(axial + step, axials), circ),
            device_id_type=MESH,
        )

    for step in range(1, circs):
        beside(step, me).start()
    out[me] = own[...]
    for step in range(1, circs):
        beside(step, axial * circs + lax.rem(circ - step + circs, circs)).wait_recv()
    for step in range(1, axials):
        along(step, axial).start()
    for step in range(1, axials):
        along(step, lax.rem(axial - step + axials, axials)).wait_recv()
    for step in range(1, circs):
        beside(step, me).wait_send()
    for step in range(1, axials):
        along(step, axial).wait_send()


def gather(own, collective_id):
    devices = lax.axis_size("axial") * lax.axis_size("circ")
    peers = lax.axis_size("axial") + lax.axis_size("circ")
    out = pl.pallas_call(
        gather_kernel,
        out_shape=jax.ShapeDtypeStruct((devices,) + own.shape, jnp.float32),
        in_specs=[VMEM],
        out_specs=VMEM,
        scratch_shapes=[
            pltpu.SemaphoreType.DMA((peers,)),
            pltpu.SemaphoreType.DMA((peers,)),
        ],
        compiler_params=params(collective_id),
        name="gather",
    )(own)
    return out.reshape(devices * LABELS, LANES)


def shifted(window, move):
    if move == 0:
        return window
    depth = window.shape[-1]
    lane = lax.broadcasted_iota(jnp.int32, window.shape, window.ndim - 1)
    rolled = pltpu.roll(window, (depth - move) % depth, window.ndim - 1)
    return jnp.where(lane == (depth - 1 if move > 0 else 0), 0.0, rolled)


def window_of(ref, x, rows_circ, offset):
    return ref[x + 1 + offset[0], PAD + offset[1] : PAD + offset[1] + rows_circ, :]


def opposite(offset):
    return (-offset[0], -offset[1], -offset[2])


def terms():
    listed = []
    for position, offset in enumerate(HALF_STEPS):
        listed.append((position, offset))
        listed.append((len(HALF_STEPS) + position, opposite(offset)))
    return sorted(listed, key=lambda term: term[1])


def in_sums(sums):
    lane = lax.broadcasted_iota(jnp.int32, (LABELS, LANES), 1)
    tile = jnp.zeros((LABELS, LANES), jnp.float32)
    for position, value in sums:
        tile = tile + jnp.where(lane == position, value, 0.0)
    return tile


def label_sums(groups_ref, field_of, rows_axial, rows_circ, depth):
    def plane(x, sums):
        labels = window_of(groups_ref, x, rows_circ, (0, 0))
        value = field_of(x)
        return tuple(
            total + jnp.where(labels == float(label), value, 0.0)
            for label, total in enumerate(sums)
        )

    blank = jnp.zeros((rows_circ, depth), jnp.float32)
    sums = lax.fori_loop(0, rows_axial, plane, (blank,) * LABELS)
    rows = [jnp.sum(total, axis=0, keepdims=True) for total in sums]
    return jnp.sum(jnp.concatenate(rows, axis=0), axis=1, keepdims=True)


def weights_kernel(ext, right, weights, panel, stiff, seen, total):
    rows_axial, rows_circ, depth = right.shape
    groups = ext.at[2]
    half = len(HALF_STEPS)

    def stiffness_plane(x, carry):
        scale = ext[0, x]
        material = ext[1, x]
        upper = material >= 8.0
        angle = material - jnp.where(upper, 8.0, 0.0)
        first = jnp.full_like(scale, 1.0)
        second = jnp.zeros_like(scale)
        for turn in range(1, 8):
            first = jnp.where(angle == float(turn), math.cos(math.pi * turn / 8.0), first)
            second = jnp.where(angle == float(turn), math.sin(math.pi * turn / 8.0), second)
        shrink = jnp.where(upper, 0.6, 1.0)
        first, second = first * shrink, second * shrink
        third = jnp.where(upper, 0.8, 0.0)
        flat = scale * jnp.where(upper, 0.35 * 0.15, 0.15)
        along = scale * jnp.where(upper, 0.35 * 2.0, 6.0)
        for position, offset in enumerate(HALF_STEPS):
            length = float(sum(part * part for part in offset))
            dot = None
            for part, line in zip(offset, (first, second, third)):
                if part != 0:
                    line = line if part > 0 else -line
                    dot = line if dot is None else dot + line
            stiff[position, x] = flat * (1.0 / length) + along * (dot * dot) * (1.0 / (length * length))
        return carry

    lax.fori_loop(0, rows_axial + 2, stiffness_plane, 0)

    def weight_plane(x, carry):
        diagonal = None
        for position, offset in enumerate(HALF_STEPS):
            field = stiff.at[position]
            centre = window_of(field, x, rows_circ, (0, 0))
            ahead = 0.5 * (centre + shifted(window_of(field, x, rows_circ, offset), offset[2]))
            back = opposite(offset)
            behind = 0.5 * (centre + shifted(window_of(field, x, rows_circ, back), back[2]))
            weights[position, x] = ahead
            weights[half + position, x] = behind
            pair = ahead + behind
            diagonal = pair if diagonal is None else diagonal + pair
        weights[2 * half, x] = MASS_SHIFT + diagonal
        return carry

    lax.fori_loop(0, rows_axial, weight_plane, 0)

    row = lax.broadcasted_iota(jnp.int32, (rows_circ, depth), 0)
    listed = terms()
    total[...] = jnp.zeros_like(total)

    def own_labels(x):
        labels = window_of(groups, x, rows_circ, (0, 0))
        return jnp.concatenate(
            [jnp.where(labels == float(label), 1.0, 0.0) for label in range(LABELS)], axis=0
        )

    def seen_labels(offset, x):
        labels = window_of(groups, x, rows_circ, offset)
        if offset[2] == 0:
            return labels
        lane = lax.broadcasted_iota(jnp.int32, labels.shape, 1)
        rolled = pltpu.roll(labels, (depth - offset[2]) % depth, 1)
        return jnp.where(lane == (depth - 1 if offset[2] > 0 else 0), -1.0, rolled)

    def add_panel(slot, x, parts):
        found = jnp.concatenate(parts, axis=0)
        total[slot] += lax.dot_general(
            own_labels(x),
            found,
            (((1,), (1,)), ((), ())),
            precision=PRECISE,
            preferred_element_type=jnp.float32,
        )

    def panel_plane(x, carry):
        for number, (position, offset) in enumerate(listed):
            labels = seen_labels(offset, x)
            leaves = None
            if offset[1] != 0:
                leaves = row == (rows_circ - 1 if offset[1] > 0 else 0)
            if offset[0] != 0:
                edge = x == (rows_axial - 1 if offset[0] > 0 else 0)
                labels = jnp.where(edge, -1.0, labels)
            seen[number] = labels if leaves is None else jnp.where(leaves, -1.0, labels)
        parts, beside = [], []
        centre = window_of(groups, x, rows_circ, (0, 0))
        for label in range(LABELS):
            found = jnp.where(centre == float(label), weights[2 * half, x], 0.0)
            for number, (position, offset) in enumerate(listed):
                found = found - jnp.where(seen[number] == float(label), weights[position, x], 0.0)
            parts.append(found)
        add_panel(0, x, parts)
        for number, (position, offset) in enumerate(listed):
            if offset[1] > 0:
                labels = seen_labels(offset, x)
                if offset[0] != 0:
                    edge = x == (rows_axial - 1 if offset[0] > 0 else 0)
                    labels = jnp.where(edge, -1.0, labels)
                seen[number] = jnp.where(row == rows_circ - 1, labels, -1.0)
        for label in range(LABELS):
            found = jnp.zeros((rows_circ, depth), jnp.float32)
            for number, (position, offset) in enumerate(listed):
                if offset[1] > 0:
                    found = found - jnp.where(
                        seen[number] == float(label), weights[position, x], 0.0
                    )
            beside.append(found)
        add_panel(1, x, beside)
        return carry

    lax.fori_loop(0, rows_axial, panel_plane, 0)

    last = rows_axial - 1
    for slot in range(2, len(PANELS)):
        move = PANELS[slot][1]
        chosen = []
        for position, offset in listed:
            if offset[0] > 0 and (offset[1] == move or move == 0):
                labels = seen_labels(offset, last)
                if offset[1] != 0:
                    leaves = row == (rows_circ - 1 if offset[1] > 0 else 0)
                    labels = jnp.where(leaves == (move != 0), labels, -1.0)
                chosen.append((position, labels))
        parts = []
        for label in range(LABELS):
            found = jnp.zeros((rows_circ, depth), jnp.float32)
            for position, labels in chosen:
                found = found - jnp.where(labels == float(label), weights[position, last], 0.0)
            parts.append(found)
        add_panel(slot, last, parts)

    size = LABELS * rows_circ
    line = lax.broadcasted_iota(jnp.int32, (size, size), 0)
    column = lax.broadcasted_iota(jnp.int32, (size, size), 1)
    same = lax.rem(line, rows_circ) == lax.rem(column, rows_circ)
    tile_row = lax.broadcasted_iota(jnp.int32, (LABELS, size), 0)
    tile_column = lax.broadcasted_iota(jnp.int32, (LABELS, size), 1)
    collect = jnp.where(tile_column // rows_circ == tile_row, 1.0, 0.0)
    spot_row = lax.broadcasted_iota(jnp.int32, (size, LANES), 0)
    spot_column = lax.broadcasted_iota(jnp.int32, (size, LANES), 1)
    result = jnp.zeros((LABELS, LANES), jnp.float32)
    for slot in range(len(PANELS)):
        lines = jnp.dot(collect, jnp.where(same, total[slot], 0.0), precision=PRECISE)
        spots = jnp.where(spot_row // rows_circ + slot * LABELS == spot_column, 1.0, 0.0)
        result = result + jnp.dot(lines, spots, precision=PRECISE)
    own = label_sums(groups, lambda x: right[x], rows_axial, rows_circ, depth)
    panel[...] = result + in_sums([(len(PANELS) * LABELS, own)])


def inverse_two(a, b, c):
    scale = 1.0 / (a * c - b * b)
    return c * scale, -b * scale, a * scale


def inverse_four(e):
    a, b, c = inverse_two(e[0][0], e[1][0], e[1][1])
    q = ((e[2][0], e[3][0]), (e[2][1], e[3][1]))
    t = [[a * q[0][k] + b * q[1][k] for k in range(2)], [b * q[0][k] + c * q[1][k] for k in range(2)]]

    def rest(i, k):
        return e[2 + max(i, k)][2 + min(i, k)] - (q[0][i] * t[0][k] + q[1][i] * t[1][k])

    x, y, z = inverse_two(rest(0, 0), rest(0, 1), rest(1, 1))
    u = [[t[i][0] * x + t[i][1] * y, t[i][0] * y + t[i][1] * z] for i in range(2)]

    def corner(i, k):
        return u[i][0] * t[k][0] + u[i][1] * t[k][1]

    across = b + corner(0, 1)
    return [
        [a + corner(0, 0), across, -u[0][0], -u[0][1]],
        [across, c + corner(1, 1), -u[1][0], -u[1][1]],
        [-u[0][0], -u[1][0], x, y],
        [-u[0][1], -u[1][1], y, z],
    ]


def inverse_of(matrices):
    size = matrices[0].shape[0]
    tiles = size // 8
    values = [matrix.reshape(tiles, 8, size) for matrix in matrices]
    lane = lax.broadcasted_iota(jnp.int32, (1, 8, size), 2)
    line = lax.broadcasted_iota(jnp.int32, (1, 8, size), 1)
    wide = (tiles, 8, size)
    for first in range(0, size, 4):
        tile, sub = first // 8, first % 8
        for number, value in enumerate(values):
            columns = [
                jnp.broadcast_to(value[:, :, first + k : first + k + 1], wide) for k in range(4)
            ]
            entries = [
                [
                    jnp.broadcast_to(columns[k][tile : tile + 1, sub + i : sub + i + 1, :], (1, 8, size))
                    for k in range(i + 1)
                ]
                for i in range(4)
            ]
            rows = []
            for i in range(4):
                row = jnp.broadcast_to(value[tile : tile + 1, sub + i : sub + i + 1, :], (1, 8, size))
                for k in range(4):
                    row = jnp.where(lane == first + k, 1.0 if i == k else 0.0, row)
                rows.append(row)
            small = inverse_four(entries)
            fresh = [
                (small[i][0] * rows[0] + small[i][1] * rows[1])
                + (small[i][2] * rows[2] + small[i][3] * rows[3])
                for i in range(4)
            ]
            inside = jnp.logical_and(lane >= first, lane < first + 4)
            left = jnp.where(inside, 0.0, value)
            left = (left - columns[0] * fresh[0] - columns[1] * fresh[1]) - (
                columns[2] * fresh[2] + columns[3] * fresh[3]
            )
            own = left[tile : tile + 1]
            for i in range(4):
                own = jnp.where(line == sub + i, fresh[i], own)
            parts = [left[:tile]] * (tile > 0) + [own] + [left[tile + 1 :]] * (tile + 1 < tiles)
            values[number] = jnp.concatenate(parts, axis=0)
    return [value.reshape(size, size) for value in values]


def coarse_kernel(cycles, gathered, inverse, diagonals, uppers, held, linked, partial):
    size = gathered.shape[0] // cycles
    whole = gathered.shape[0]
    circs = size // LABELS
    line = lax.broadcasted_iota(jnp.int32, (size, size), 0) // LABELS
    column = lax.broadcasted_iota(jnp.int32, (size, size), 1) // LABELS
    spread_row = lax.broadcasted_iota(jnp.int32, (LANES, size), 0)
    spread_column = lax.rem(lax.broadcasted_iota(jnp.int32, (LANES, size), 1), LABELS)

    def dot(left, right):
        return jnp.dot(left, right, precision=PRECISE, preferred_element_type=jnp.float32)

    def block(s, slot):
        tiles = jnp.where(spread_row == spread_column + slot * LABELS, 1.0, 0.0)
        placed = dot(gathered[pl.ds(s * size, size), :], tiles)
        return jnp.where(lax.rem(line + PANELS[slot][1] + circs, circs) == column, placed, 0.0)

    def assemble(s, carry):
        beside = block(s, 1)
        diagonals[s] = block(s, 0) + beside + beside.T
        uppers[s] = block(s, 2) + block(s, 3) + block(s, 4)
        return carry

    lax.fori_loop(0, cycles, assemble, 0)
    unit_line = lax.broadcasted_iota(jnp.int32, (size, whole), 0)
    unit_column = lax.broadcasted_iota(jnp.int32, (size, whole), 1)

    def unit(s):
        return jnp.where(unit_line + s * size == unit_column, 1.0, 0.0)

    def eliminate(s, s_next, upper):
        inverted = inverse_of([diagonals[s]])[0]
        link = dot(inverted, upper)
        held[s] = inverted
        linked[s] = link
        across = upper.T
        diagonals[s_next] = diagonals[s_next] - dot(across, link)
        partial[s_next] = partial[s_next] - dot(link.T, partial[s])

    def start(s, carry):
        partial[s] = unit(s)
        return carry

    lax.fori_loop(0, cycles, start, 0)
    middle = cycles // 2

    def from_both_ends(step, carry):
        low, high = step, cycles - 1 - step
        upper_low, upper_high = uppers[low], uppers[high - 1].T
        inverted_low, inverted_high = inverse_of([diagonals[low], diagonals[high]])
        for s, s_next, upper, inverted in (
            (low, low + 1, upper_low, inverted_low),
            (high, high - 1, upper_high, inverted_high),
        ):
            link = dot(inverted, upper)
            held[s] = inverted
            linked[s] = link
            diagonals[s_next] = diagonals[s_next] - dot(upper.T, link)
            partial[s_next] = partial[s_next] - dot(link.T, partial[s])
        return carry

    lax.fori_loop(0, middle - 1, from_both_ends, 0)
    eliminate(middle - 1, middle, uppers[middle - 1])
    rows = pl.ds(middle * size, size)
    inverse[rows, :] = dot(inverse_of([diagonals[middle]])[0], partial[middle])

    def put(s, s_next):
        ahead = inverse[pl.ds(s_next * size, size), :]
        inverse[pl.ds(s * size, size), :] = dot(held[s], partial[s]) - dot(linked[s], ahead)

    put(middle - 1, middle)

    def back(step, carry):
        put(middle - 2 - step, middle - 1 - step)
        put(middle + 1 + step, middle + step)
        return carry

    lax.fori_loop(0, middle - 1, back, 0)


def coarse_inverse(gathered):
    cycles, circs = lax.axis_size("axial"), lax.axis_size("circ")
    size, whole = circs * LABELS, gathered.shape[0]
    square = pltpu.VMEM((cycles, size, size), jnp.float32)
    return pl.pallas_call(
        functools.partial(coarse_kernel, cycles),
        out_shape=jax.ShapeDtypeStruct((whole, whole), jnp.float32),
        in_specs=[VMEM],
        out_specs=VMEM,
        scratch_shapes=[square] * 4 + [pltpu.VMEM((cycles, size, whole), jnp.float32)],
        compiler_params=params(),
        name="coarse_inverse",
    )(gathered)


def apply_plane(ext, weights, x, rows_circ):
    centre = 2 * len(HALF_STEPS)
    result = weights[centre, x] * window_of(ext, x, rows_circ, (0, 0))
    for position, offset in terms():
        value = shifted(window_of(ext, x, rows_circ, offset), offset[2])
        result = result - weights[position, x] * value
    return result


def spread_into(spread, values, column, groups):
    planes, rows, depth = spread.shape
    axials, circs = lax.axis_size("axial"), lax.axis_size("circ")
    axial, circ = lax.axis_index("axial"), lax.axis_index("circ")
    row = lax.broadcasted_iota(jnp.int32, (rows, depth), 0)

    def tile(a, c):
        at = axial + a
        present = jnp.logical_and(at >= 0, at < axials)
        at = jnp.minimum(jnp.maximum(at, 0), axials - 1)
        number = at * circs + lax.rem(circ + c + circs, circs)
        part = values[pl.ds(pl.multiple_of(number * LABELS, LABELS), LABELS), column : column + 1]
        return jnp.where(present, jnp.broadcast_to(part, (LABELS, depth)), 0.0)

    def fill(x, sides):
        labels = groups[x]
        value = jnp.zeros((rows, depth), jnp.float32)
        for label in range(LABELS):
            before, here, after = [side[label : label + 1, :] for side in sides]
            chosen = jnp.where(row < PAD, before, jnp.where(row < rows - PAD, here, after))
            value = jnp.where(labels == float(label), chosen, value)
        spread[x] = value

    fill(0, [tile(-1, c) for c in (-1, 0, 1)])
    fill(planes - 1, [tile(1, c) for c in (-1, 0, 1)])
    sides = [tile(0, c) for c in (-1, 0, 1)]

    def inner(x, carry):
        fill(x, sides)
        return carry

    lax.fori_loop(1, planes - 1, inner, 0)


def start_kernel(inverse, gathered, ext, weights, right, solution, residual, values, spread):
    rows_axial, rows_circ, depth = right.shape
    values[...] = jnp.dot(inverse[...], gathered[...], precision=PRECISE)
    spread_into(spread, values, len(PANELS) * LABELS, ext.at[2])

    def plane(x, carry):
        solution[x] = window_of(spread, x, rows_circ, (0, 0))
        residual[x] = right[x] - apply_plane(spread, weights, x, rows_circ)
        return carry

    lax.fori_loop(0, rows_axial, plane, 0)


def image_kernel(later, *refs):
    if later:
        residual_ext, ext, weights, direction_image, image, sums = refs
    else:
        residual_ext, ext, weights, image, sums = refs
    rows_axial, rows_circ, depth = image.shape
    field = residual_ext.at[0]

    def plane(x, totals):
        value = apply_plane(field, weights, x, rows_circ)
        image[x] = value
        residual = window_of(field, x, rows_circ, (0, 0))
        factors = [residual, value] + ([direction_image[x]] if later else [])
        return tuple(total + residual * factor for total, factor in zip(totals, factors))

    blank = jnp.zeros((rows_circ, depth), jnp.float32)
    totals = lax.fori_loop(0, rows_axial, plane, (blank,) * (3 if later else 2))
    found = [(0, label_sums(ext.at[2], lambda x: image[x], rows_axial, rows_circ, depth))]
    line = lax.broadcasted_iota(jnp.int32, (LABELS, LANES), 0)
    for position, total in enumerate(totals):
        whole = jnp.sum(jnp.sum(total, axis=0, keepdims=True), axis=1, keepdims=True)
        found.append((position + 1, jnp.where(line == 0, whole, 0.0)))
    sums[...] = in_sums(found)


def update_kernel(later, final, *refs):
    inverse, gathered, ext, weights, solution, residual, image = refs[:7]
    refs = refs[7:]
    if later:
        direction, direction_image, scalars = refs[:3]
        refs = refs[3:]
    solution_out, residual_out = refs[:2]
    refs = refs[2:]
    if not final:
        direction_out, direction_image_out, scalars_out = refs[:3]
        refs = refs[3:]
    values, spread = refs
    rows_axial, rows_circ, depth = solution.shape
    values[...] = jnp.dot(inverse[...], gathered[...], precision=PRECISE)
    spread_into(spread, values, 0, ext.at[2])
    totals = jnp.sum(gathered[...], axis=0, keepdims=True)
    norm = totals[:, 1:2]
    overlap = jnp.sum(gathered[...] * values[...], axis=0, keepdims=True)[:, 0:1]
    curvature = totals[:, 2:3] - overlap
    if later:
        ratio = norm / scalars[0:1, 0:1]
        curvature = ratio * ratio * scalars[0:1, 1:2] + 2.0 * ratio * totals[:, 3:4] + curvature
    step = norm / curvature

    def plane(x, carry):
        now = residual[x]
        along = now - window_of(spread, x, rows_circ, (0, 0))
        along_image = image[x] - apply_plane(spread, weights, x, rows_circ)
        if later:
            along = along + ratio * direction[x]
            along_image = along_image + ratio * direction_image[x]
        solution_out[x] = solution[x] + step * along
        residual_out[x] = now - step * along_image
        if not final:
            direction_out[x] = along
            direction_image_out[x] = along_image
        return carry

    lax.fori_loop(0, rows_axial, plane, 0)
    if not final:
        scalars_out[...] = in_sums([(0, norm), (1, curvature)])


def call(kernel, outs, scratch, args, name):
    return pl.pallas_call(
        kernel,
        out_shape=[jax.ShapeDtypeStruct(shape, jnp.float32) for shape in outs],
        in_specs=[VMEM] * len(args),
        out_specs=[VMEM] * len(outs),
        scratch_shapes=[pltpu.VMEM(shape, jnp.float32) for shape in scratch],
        compiler_params=params(),
        name=name,
    )(*args)


def shards(right_side, stiffness, material, groups):
    block = right_side.shape
    rows_axial, rows_circ, depth = block
    padded = (rows_axial + 2, rows_circ + 2 * PAD, depth)
    count = 2 * len(HALF_STEPS) + 1
    tile = (LABELS, LANES)
    size = LABELS * rows_circ
    ext = halo([stiffness, material, groups], 0)
    weights, panel = call(
        weights_kernel,
        [(count,) + block, tile],
        [(len(HALF_STEPS),) + padded, (count, rows_circ, depth), (len(PANELS), size, size)],
        [ext, right_side],
        "weights",
    )
    gathered = gather(panel, 1)
    inverse = coarse_inverse(gathered)
    work = [gathered.shape, padded]
    solution, residual = call(
        start_kernel, [block, block], work, [inverse, gathered, ext, weights, right_side], "start"
    )
    carried = []
    for iteration in range(ITERS):
        later, final = iteration > 0, iteration + 1 == ITERS
        residual_ext = halo([residual], 2 + 2 * iteration)
        image, sums = call(
            functools.partial(image_kernel, later),
            [block, tile],
            [],
            [residual_ext, ext, weights] + carried[1:2],
            "image",
        )
        gathered = gather(sums, 3 + 2 * iteration)
        solution, residual, *carried = call(
            functools.partial(update_kernel, later, final),
            [block, block] + ([] if final else [block, block, tile]),
            work,
            [inverse, gathered, ext, weights, solution, residual, image] + carried,
            "update",
        )
    return (solution, residual)


def solution(mesh):
    in_specs = (
        P("axial", "circ", None),
        P("axial", "circ", None),
        P("axial", "circ", None),
        P("axial", "circ", None),
    )
    out_specs = (P("axial", "circ", None), P("axial", "circ", None))
    return jax.shard_map(shards, mesh=mesh, in_specs=in_specs, out_specs=out_specs, check_vma=False)
```

```python
import functools
import math

import jax
import jax.numpy as jnp
from jax import lax
from jax.experimental import pallas as pl
from jax.experimental.pallas import tpu as pltpu
from jax.sharding import PartitionSpec as P

LABELS = 8
ITERS = 2
MASS_SHIFT = 0.02
PRECISE = lax.Precision.HIGHEST
MESH = pl.DeviceIdType.MESH
PAD = 8
LANES = 128
VMEM = pl.BlockSpec(memory_space=pltpu.VMEM)
HALF_STEPS = (
    (0, 0, 1),
    (0, 1, -1),
    (0, 1, 0),
    (0, 1, 1),
    (1, -1, -1),
    (1, -1, 0),
    (1, -1, 1),
    (1, 0, -1),
    (1, 0, 0),
    (1, 0, 1),
    (1, 1, -1),
    (1, 1, 0),
    (1, 1, 1),
)


SIDES = tuple((a, c) for a in (-1, 0, 1) for c in (-1, 0, 1) if (a, c) != (0, 0))
PANELS = ((0, 0), (0, 1), (1, -1), (1, 0), (1, 1))


def params(collective_id=None):
    if collective_id is None:
        return pltpu.CompilerParams(vmem_limit_bytes=56 * 1024 * 1024)
    return pltpu.CompilerParams(
        vmem_limit_bytes=56 * 1024 * 1024, collective_id=collective_id, has_side_effects=True
    )


def wrapped(value, length):
    return value - jnp.where(value >= length, length, 0)


def for_others(action):
    axials, circs = lax.axis_size("axial"), lax.axis_size("circ")
    for c in range(1, circs):
        action(0, c)

    def row(a, carry):
        for c in range(circs):
            action(a, c)
        return carry

    lax.fori_loop(1, axials, row, 0)


def other(a, c):
    axials, circs = lax.axis_size("axial"), lax.axis_size("circ")
    return (
        wrapped(lax.axis_index("axial") + a, axials),
        wrapped(lax.axis_index("circ") + c, circs),
    )


def greet():
    barrier = pltpu.get_barrier_semaphore()

    def signal(a, c):
        pl.semaphore_signal(barrier, inc=1, device_id=other(a, c), device_id_type=MESH)

    for_others(signal)


def greeted():
    devices = lax.axis_size("axial") * lax.axis_size("circ")
    pl.semaphore_wait(pltpu.get_barrier_semaphore(), devices - 1)


def inside(move):
    at = lax.axis_index("axial") + move
    return jnp.logical_and(at >= 0, at < lax.axis_size("axial"))


def halo_buffers(count, block):
    rows_axial, rows_circ, depth = block
    buffers = [
        pltpu.VMEM((2, count, rows_axial, depth), jnp.float32),
        pltpu.VMEM((2, count, rows_circ, depth), jnp.float32),
        pltpu.VMEM((4, count, 1, depth), jnp.float32),
    ]
    return buffers + buffers + [pltpu.SemaphoreType.DMA((len(SIDES),))] * 2


def halo_copy(side, refs):
    send_circ, send_axial, send_corner, recv_circ, recv_axial, recv_corner, send_sem, recv_sem = refs
    circs = lax.axis_size("circ")
    a, c = (side[0] + 1) // 2, (side[1] + 1) // 2
    if side[0] == 0:
        source, target = send_circ.at[c], recv_circ.at[1 - c]
    elif side[1] == 0:
        source, target = send_axial.at[a], recv_axial.at[1 - a]
    else:
        source, target = send_corner.at[2 * a + c], recv_corner.at[3 - 2 * a - c]
    number = SIDES.index(side)
    return pltpu.make_async_remote_copy(
        src_ref=source,
        dst_ref=target,
        send_sem=send_sem.at[number],
        recv_sem=recv_sem.at[number],
        device_id=(
            lax.axis_index("axial") + side[0],
            wrapped(lax.axis_index("circ") + side[1] % circs, circs),
        ),
        device_id_type=MESH,
    )


def halo_send(fields, refs):
    send_circ, send_axial, send_corner = refs[:3]
    rows_axial, rows_circ, depth = fields[0].shape
    for f, field in enumerate(fields):
        for a in range(2):
            x = a * (rows_axial - 1)
            send_axial[a, f] = field[x].astype(jnp.float32)
            for c in range(2):
                row = c * (rows_circ - 1)
                send_corner[2 * a + c, f] = field[x, row : row + 1, :].astype(jnp.float32)
        for c in range(2):
            row = c * (rows_circ - 1)
            for x in range(rows_axial):
                send_circ[c, f, x : x + 1, :] = field[x, row : row + 1, :].astype(jnp.float32)
    greeted()
    for side in SIDES:
        @pl.when(inside(side[0]))
        def _():
            halo_copy(side, refs).start()


def halo_fill(fields, out):
    rows_axial, rows_circ, depth = fields[0].shape
    for f, field in enumerate(fields):
        for x in (0, rows_axial + 1):
            out[f, x] = jnp.zeros((rows_circ + 2 * PAD, depth), jnp.float32)
        blank = jnp.zeros((rows_axial, PAD, depth), jnp.float32)
        out[f, 1 : rows_axial + 1, 0:PAD, :] = blank
        out[f, 1 : rows_axial + 1, PAD + rows_circ :, :] = blank
        out[f, 1 : rows_axial + 1, PAD : PAD + rows_circ, :] = field[...].astype(jnp.float32)


def halo_receive(fields, out, refs):
    recv_circ, recv_axial, recv_corner = refs[3:6]
    rows_axial, rows_circ, depth = fields[0].shape
    count = len(fields)
    edge = (PAD - 1, PAD + rows_circ)
    for side in SIDES:
        a, c = (1 - side[0]) // 2, (1 - side[1]) // 2
        x = a * (rows_axial + 1)

        @pl.when(inside(-side[0]))
        def _():
            halo_copy(side, refs).wait_recv()
            for f in range(count):
                if side[0] == 0:
                    for row in range(rows_axial):
                        out[f, row + 1, edge[c] : edge[c] + 1, :] = recv_circ[c, f, row : row + 1, :]
                elif side[1] == 0:
                    out[f, x, PAD : PAD + rows_circ, :] = recv_axial[a, f]
                else:
                    out[f, x, edge[c] : edge[c] + 1, :] = recv_corner[2 * a + c, f]

    for side in SIDES:
        @pl.when(inside(side[0]))
        def _():
            halo_copy(side, refs).wait_send()


def gather(own, out, send_sem, recv_sem):
    axials, circs = lax.axis_size("axial"), lax.axis_size("circ")
    me = lax.axis_index("axial") * circs + lax.axis_index("circ")

    def send(a, c):
        pltpu.make_async_remote_copy(
            src_ref=own,
            dst_ref=out.at[me],
            send_sem=send_sem,
            recv_sem=recv_sem,
            device_id=other(a, c),
            device_id_type=MESH,
        ).start()

    for_others(send)
    out[me] = own[...]
    most = out.at[pl.ds(0, axials * circs - 1)]
    everything = pltpu.make_async_remote_copy(
        src_ref=most,
        dst_ref=most,
        send_sem=send_sem,
        recv_sem=recv_sem,
        device_id=other(0, 1),
        device_id_type=MESH,
    )
    everything.wait_recv()
    everything.wait_send()


def shifted(window, move):
    if move == 0:
        return window
    depth = window.shape[-1]
    lane = lax.broadcasted_iota(jnp.int32, window.shape, window.ndim - 1)
    rolled = pltpu.roll(window, (depth - move) % depth, window.ndim - 1)
    return jnp.where(lane == (depth - 1 if move > 0 else 0), 0.0, rolled)


def window_of(ref, x, rows_circ, offset):
    return ref[x + 1 + offset[0], PAD + offset[1] : PAD + offset[1] + rows_circ, :]


def opposite(offset):
    return (-offset[0], -offset[1], -offset[2])


def terms():
    listed = []
    for position, offset in enumerate(HALF_STEPS):
        listed.append((position, offset))
        listed.append((len(HALF_STEPS) + position, opposite(offset)))
    return sorted(listed, key=lambda term: term[1])


def in_sums(sums):
    lane = lax.broadcasted_iota(jnp.int32, (LABELS, LANES), 1)
    tile = jnp.zeros((LABELS, LANES), jnp.float32)
    for position, value in sums:
        tile = tile + jnp.where(lane == position, value, 0.0)
    return tile


def label_sums(groups_ref, field_of, rows_axial, rows_circ, depth):
    def plane(x, sums):
        labels = window_of(groups_ref, x, rows_circ, (0, 0))
        value = field_of(x)
        return tuple(
            total + jnp.where(labels == float(label), value, 0.0)
            for label, total in enumerate(sums)
        )

    blank = jnp.zeros((rows_circ, depth), jnp.float32)
    sums = lax.fori_loop(0, rows_axial, plane, (blank,) * LABELS)
    rows = [jnp.sum(total, axis=0, keepdims=True) for total in sums]
    return jnp.sum(jnp.concatenate(rows, axis=0), axis=1, keepdims=True)


def weights_kernel(stiffness, material_ref, groups_ref, right, ext, weights, gathered, panel, stiff, seen, total, gather_send, gather_recv, *halo_refs):
    rows_axial, rows_circ, depth = right.shape
    greet()
    fields = (stiffness, material_ref, groups_ref)
    halo_send(fields, halo_refs)
    halo_fill(fields, ext)
    own = label_sums(ext.at[2], lambda x: right[x], rows_axial, rows_circ, depth)
    halo_receive(fields, ext, halo_refs)
    groups = ext.at[2]
    half = len(HALF_STEPS)

    def stiffness_plane(x, carry):
        scale = ext[0, x]
        material = ext[1, x]
        upper = material >= 8.0
        angle = material - jnp.where(upper, 8.0, 0.0)
        first = jnp.full_like(scale, 1.0)
        second = jnp.zeros_like(scale)
        for turn in range(1, 8):
            first = jnp.where(angle == float(turn), math.cos(math.pi * turn / 8.0), first)
            second = jnp.where(angle == float(turn), math.sin(math.pi * turn / 8.0), second)
        shrink = jnp.where(upper, 0.6, 1.0)
        first, second = first * shrink, second * shrink
        third = jnp.where(upper, 0.8, 0.0)
        flat = scale * jnp.where(upper, 0.35 * 0.15, 0.15)
        along = scale * jnp.where(upper, 0.35 * 2.0, 6.0)
        for position, offset in enumerate(HALF_STEPS):
            length = float(sum(part * part for part in offset))
            dot = None
            for part, line in zip(offset, (first, second, third)):
                if part != 0:
                    line = line if part > 0 else -line
                    dot = line if dot is None else dot + line
            stiff[position, x] = flat * (1.0 / length) + along * (dot * dot) * (1.0 / (length * length))
        return carry

    lax.fori_loop(0, rows_axial + 2, stiffness_plane, 0)

    def weight_plane(x, carry):
        diagonal = None
        for position, offset in enumerate(HALF_STEPS):
            field = stiff.at[position]
            centre = window_of(field, x, rows_circ, (0, 0))
            ahead = 0.5 * (centre + shifted(window_of(field, x, rows_circ, offset), offset[2]))
            back = opposite(offset)
            behind = 0.5 * (centre + shifted(window_of(field, x, rows_circ, back), back[2]))
            weights[position, x] = ahead
            weights[half + position, x] = behind
            pair = ahead + behind
            diagonal = pair if diagonal is None else diagonal + pair
        weights[2 * half, x] = MASS_SHIFT + diagonal
        return carry

    lax.fori_loop(0, rows_axial, weight_plane, 0)

    row = lax.broadcasted_iota(jnp.int32, (rows_circ, depth), 0)
    listed = terms()
    total[...] = jnp.zeros_like(total)

    def own_labels(x):
        labels = window_of(groups, x, rows_circ, (0, 0))
        return jnp.concatenate(
            [jnp.where(labels == float(label), 1.0, 0.0) for label in range(LABELS)], axis=0
        )

    def seen_labels(offset, x):
        labels = window_of(groups, x, rows_circ, offset)
        if offset[2] == 0:
            return labels
        lane = lax.broadcasted_iota(jnp.int32, labels.shape, 1)
        rolled = pltpu.roll(labels, (depth - offset[2]) % depth, 1)
        return jnp.where(lane == (depth - 1 if offset[2] > 0 else 0), -1.0, rolled)

    def add_panel(slot, x, parts):
        found = jnp.concatenate(parts, axis=0)
        total[slot] += lax.dot_general(
            own_labels(x),
            found,
            (((1,), (1,)), ((), ())),
            precision=PRECISE,
            preferred_element_type=jnp.float32,
        )

    def panel_plane(x, carry):
        for number, (position, offset) in enumerate(listed):
            labels = seen_labels(offset, x)
            leaves = None
            if offset[1] != 0:
                leaves = row == (rows_circ - 1 if offset[1] > 0 else 0)
            if offset[0] != 0:
                edge = x == (rows_axial - 1 if offset[0] > 0 else 0)
                labels = jnp.where(edge, -1.0, labels)
            seen[number] = labels if leaves is None else jnp.where(leaves, -1.0, labels)
        parts, beside = [], []
        centre = window_of(groups, x, rows_circ, (0, 0))
        for label in range(LABELS):
            found = jnp.where(centre == float(label), weights[2 * half, x], 0.0)
            for number, (position, offset) in enumerate(listed):
                found = found - jnp.where(seen[number] == float(label), weights[position, x], 0.0)
            parts.append(found)
        add_panel(0, x, parts)
        for number, (position, offset) in enumerate(listed):
            if offset[1] > 0:
                labels = seen_labels(offset, x)
                if offset[0] != 0:
                    edge = x == (rows_axial - 1 if offset[0] > 0 else 0)
                    labels = jnp.where(edge, -1.0, labels)
                seen[number] = jnp.where(row == rows_circ - 1, labels, -1.0)
        for label in range(LABELS):
            found = jnp.zeros((rows_circ, depth), jnp.float32)
            for number, (position, offset) in enumerate(listed):
                if offset[1] > 0:
                    found = found - jnp.where(
                        seen[number] == float(label), weights[position, x], 0.0
                    )
            beside.append(found)
        add_panel(1, x, beside)
        return carry

    lax.fori_loop(0, rows_axial, panel_plane, 0)

    last = rows_axial - 1
    for slot in range(2, len(PANELS)):
        move = PANELS[slot][1]
        chosen = []
        for position, offset in listed:
            if offset[0] > 0 and (offset[1] == move or move == 0):
                labels = seen_labels(offset, last)
                if offset[1] != 0:
                    leaves = row == (rows_circ - 1 if offset[1] > 0 else 0)
                    labels = jnp.where(leaves == (move != 0), labels, -1.0)
                chosen.append((position, labels))
        parts = []
        for label in range(LABELS):
            found = jnp.zeros((rows_circ, depth), jnp.float32)
            for position, labels in chosen:
                found = found - jnp.where(labels == float(label), weights[position, last], 0.0)
            parts.append(found)
        add_panel(slot, last, parts)

    size = LABELS * rows_circ
    line = lax.broadcasted_iota(jnp.int32, (size, size), 0)
    column = lax.broadcasted_iota(jnp.int32, (size, size), 1)
    same = lax.rem(line, rows_circ) == lax.rem(column, rows_circ)
    tile_row = lax.broadcasted_iota(jnp.int32, (LABELS, size), 0)
    tile_column = lax.broadcasted_iota(jnp.int32, (LABELS, size), 1)
    collect = jnp.where(tile_column // rows_circ == tile_row, 1.0, 0.0)
    spot_row = lax.broadcasted_iota(jnp.int32, (size, LANES), 0)
    spot_column = lax.broadcasted_iota(jnp.int32, (size, LANES), 1)
    result = jnp.zeros((LABELS, LANES), jnp.float32)
    for slot in range(len(PANELS)):
        lines = jnp.dot(collect, jnp.where(same, total[slot], 0.0), precision=PRECISE)
        spots = jnp.where(spot_row // rows_circ + slot * LABELS == spot_column, 1.0, 0.0)
        result = result + jnp.dot(lines, spots, precision=PRECISE)
    panel[...] = result + in_sums([(len(PANELS) * LABELS, own)])
    gather(panel, gathered, gather_send, gather_recv)


def inverse_two(a, b, c):
    scale = 1.0 / (a * c - b * b)
    return c * scale, -b * scale, a * scale


def inverse_four(e):
    a, b, c = inverse_two(e[0][0], e[1][0], e[1][1])
    q = ((e[2][0], e[3][0]), (e[2][1], e[3][1]))
    t = [[a * q[0][k] + b * q[1][k] for k in range(2)], [b * q[0][k] + c * q[1][k] for k in range(2)]]

    def rest(i, k):
        return e[2 + max(i, k)][2 + min(i, k)] - (q[0][i] * t[0][k] + q[1][i] * t[1][k])

    x, y, z = inverse_two(rest(0, 0), rest(0, 1), rest(1, 1))
    u = [[t[i][0] * x + t[i][1] * y, t[i][0] * y + t[i][1] * z] for i in range(2)]

    def corner(i, k):
        return u[i][0] * t[k][0] + u[i][1] * t[k][1]

    across = b + corner(0, 1)
    return [
        [a + corner(0, 0), across, -u[0][0], -u[0][1]],
        [across, c + corner(1, 1), -u[1][0], -u[1][1]],
        [-u[0][0], -u[1][0], x, y],
        [-u[0][1], -u[1][1], y, z],
    ]


def inverse_of(matrices):
    size = matrices[0].shape[0]
    tiles = size // 8
    values = [matrix.reshape(tiles, 8, size) for matrix in matrices]
    lane = lax.broadcasted_iota(jnp.int32, (1, 8, size), 2)
    line = lax.broadcasted_iota(jnp.int32, (1, 8, size), 1)
    wide = (tiles, 8, size)
    for first in range(0, size, 4):
        tile, sub = first // 8, first % 8
        for number, value in enumerate(values):
            columns = [
                jnp.broadcast_to(value[:, :, first + k : first + k + 1], wide) for k in range(4)
            ]
            entries = [
                [
                    jnp.broadcast_to(columns[k][tile : tile + 1, sub + i : sub + i + 1, :], (1, 8, size))
                    for k in range(i + 1)
                ]
                for i in range(4)
            ]
            rows = []
            for i in range(4):
                row = jnp.broadcast_to(value[tile : tile + 1, sub + i : sub + i + 1, :], (1, 8, size))
                for k in range(4):
                    row = jnp.where(lane == first + k, 1.0 if i == k else 0.0, row)
                rows.append(row)
            small = inverse_four(entries)
            fresh = [
                (small[i][0] * rows[0] + small[i][1] * rows[1])
                + (small[i][2] * rows[2] + small[i][3] * rows[3])
                for i in range(4)
            ]
            inside = jnp.logical_and(lane >= first, lane < first + 4)
            left = jnp.where(inside, 0.0, value)
            left = (left - columns[0] * fresh[0] - columns[1] * fresh[1]) - (
                columns[2] * fresh[2] + columns[3] * fresh[3]
            )
            own = left[tile : tile + 1]
            for i in range(4):
                own = jnp.where(line == sub + i, fresh[i], own)
            parts = [left[:tile]] * (tile > 0) + [own] + [left[tile + 1 :]] * (tile + 1 < tiles)
            values[number] = jnp.concatenate(parts, axis=0)
    return [value.reshape(size, size) for value in values]


def coarse_kernel(cycles, gathered, inverse, diagonals, uppers, held, linked, partial):
    size = gathered.shape[0] // cycles
    whole = gathered.shape[0]
    circs = size // LABELS
    line = lax.broadcasted_iota(jnp.int32, (size, size), 0) // LABELS
    column = lax.broadcasted_iota(jnp.int32, (size, size), 1) // LABELS
    spread_row = lax.broadcasted_iota(jnp.int32, (LANES, size), 0)
    spread_column = lax.rem(lax.broadcasted_iota(jnp.int32, (LANES, size), 1), LABELS)

    def dot(left, right):
        return jnp.dot(left, right, precision=PRECISE, preferred_element_type=jnp.float32)

    def block(s, slot):
        tiles = jnp.where(spread_row == spread_column + slot * LABELS, 1.0, 0.0)
        placed = dot(gathered[pl.ds(s * size, size), :], tiles)
        return jnp.where(lax.rem(line + PANELS[slot][1] + circs, circs) == column, placed, 0.0)

    def assemble(s, carry):
        beside = block(s, 1)
        diagonals[s] = block(s, 0) + beside + beside.T
        uppers[s] = block(s, 2) + block(s, 3) + block(s, 4)
        return carry

    lax.fori_loop(0, cycles, assemble, 0)
    unit_line = lax.broadcasted_iota(jnp.int32, (size, whole), 0)
    unit_column = lax.broadcasted_iota(jnp.int32, (size, whole), 1)

    def unit(s):
        return jnp.where(unit_line + s * size == unit_column, 1.0, 0.0)

    def eliminate(s, s_next, upper):
        inverted = inverse_of([diagonals[s]])[0]
        link = dot(inverted, upper)
        held[s] = inverted
        linked[s] = link
        across = upper.T
        diagonals[s_next] = diagonals[s_next] - dot(across, link)
        partial[s_next] = partial[s_next] - dot(link.T, partial[s])

    def start(s, carry):
        partial[s] = unit(s)
        return carry

    lax.fori_loop(0, cycles, start, 0)
    middle = cycles // 2

    def from_both_ends(step, carry):
        low, high = step, cycles - 1 - step
        upper_low, upper_high = uppers[low], uppers[high - 1].T
        inverted_low, inverted_high = inverse_of([diagonals[low], diagonals[high]])
        for s, s_next, upper, inverted in (
            (low, low + 1, upper_low, inverted_low),
            (high, high - 1, upper_high, inverted_high),
        ):
            link = dot(inverted, upper)
            held[s] = inverted
            linked[s] = link
            diagonals[s_next] = diagonals[s_next] - dot(upper.T, link)
            partial[s_next] = partial[s_next] - dot(link.T, partial[s])
        return carry

    lax.fori_loop(0, middle - 1, from_both_ends, 0)
    eliminate(middle - 1, middle, uppers[middle - 1])
    rows = pl.ds(middle * size, size)
    inverse[rows, :] = dot(inverse_of([diagonals[middle]])[0], partial[middle])

    def put(s, s_next):
        ahead = inverse[pl.ds(s_next * size, size), :]
        inverse[pl.ds(s * size, size), :] = dot(held[s], partial[s]) - dot(linked[s], ahead)

    put(middle - 1, middle)

    def back(step, carry):
        put(middle - 2 - step, middle - 1 - step)
        put(middle + 1 + step, middle + step)
        return carry

    lax.fori_loop(0, middle - 1, back, 0)


def coarse_inverse(gathered):
    cycles, circs = lax.axis_size("axial"), lax.axis_size("circ")
    size, whole = circs * LABELS, gathered.shape[0]
    square = pltpu.VMEM((cycles, size, size), jnp.float32)
    return pl.pallas_call(
        functools.partial(coarse_kernel, cycles),
        out_shape=jax.ShapeDtypeStruct((whole, whole), jnp.float32),
        in_specs=[VMEM],
        out_specs=VMEM,
        scratch_shapes=[square] * 4 + [pltpu.VMEM((cycles, size, whole), jnp.float32)],
        compiler_params=params(),
        name="coarse_inverse",
    )(gathered)


def apply_plane(ext, weights, x, rows_circ):
    centre = 2 * len(HALF_STEPS)
    result = weights[centre, x] * window_of(ext, x, rows_circ, (0, 0))
    for position, offset in terms():
        value = shifted(window_of(ext, x, rows_circ, offset), offset[2])
        result = result - weights[position, x] * value
    return result


def spread_into(spread, values, column, groups):
    planes, rows, depth = spread.shape
    axials, circs = lax.axis_size("axial"), lax.axis_size("circ")
    axial, circ = lax.axis_index("axial"), lax.axis_index("circ")
    row = lax.broadcasted_iota(jnp.int32, (rows, depth), 0)

    def tile(a, c):
        at = axial + a
        present = jnp.logical_and(at >= 0, at < axials)
        at = jnp.minimum(jnp.maximum(at, 0), axials - 1)
        number = at * circs + lax.rem(circ + c + circs, circs)
        part = values[pl.ds(pl.multiple_of(number * LABELS, LABELS), LABELS), column : column + 1]
        return jnp.where(present, jnp.broadcast_to(part, (LABELS, depth)), 0.0)

    def fill(x, sides):
        labels = groups[x]
        value = jnp.zeros((rows, depth), jnp.float32)
        for label in range(LABELS):
            before, here, after = [side[label : label + 1, :] for side in sides]
            chosen = jnp.where(row < PAD, before, jnp.where(row < rows - PAD, here, after))
            value = jnp.where(labels == float(label), chosen, value)
        spread[x] = value

    fill(0, [tile(-1, c) for c in (-1, 0, 1)])
    fill(planes - 1, [tile(1, c) for c in (-1, 0, 1)])
    sides = [tile(0, c) for c in (-1, 0, 1)]

    def inner(x, carry):
        fill(x, sides)
        return carry

    lax.fori_loop(1, planes - 1, inner, 0)


def start_kernel(inverse, gathered, ext, weights, right, solution, residual, image, sums_out, *refs):
    values, spread, field, sums = refs[:4]
    rows_axial, rows_circ, depth = right.shape
    greet()
    values[...] = jnp.dot(inverse[...], gathered[...], precision=PRECISE)
    spread_into(spread, values, len(PANELS) * LABELS, ext.at[2])

    def plane(x, carry):
        solution[x] = window_of(spread, x, rows_circ, (0, 0))
        residual[x] = right[x] - apply_plane(spread, weights, x, rows_circ)
        return carry

    lax.fori_loop(0, rows_axial, plane, 0)
    image_sums(residual, field, ext, weights, None, image, sums, sums_out, refs[4:])


def image_sums(residual_ref, field_ext, ext, weights, direction_image, image, sums, sums_out, refs):
    later = direction_image is not None
    halo_send((residual_ref,), refs[2:])
    halo_fill((residual_ref,), field_ext)
    halo_receive((residual_ref,), field_ext, refs[2:])
    rows_axial, rows_circ, depth = image.shape
    field = field_ext.at[0]

    def plane(x, totals):
        value = apply_plane(field, weights, x, rows_circ)
        image[x] = value
        residual = window_of(field, x, rows_circ, (0, 0))
        factors = [residual, value] + ([direction_image[x]] if later else [])
        return tuple(total + residual * factor for total, factor in zip(totals, factors))

    blank = jnp.zeros((rows_circ, depth), jnp.float32)
    totals = lax.fori_loop(0, rows_axial, plane, (blank,) * (3 if later else 2))
    found = [(0, label_sums(ext.at[2], lambda x: image[x], rows_axial, rows_circ, depth))]
    line = lax.broadcasted_iota(jnp.int32, (LABELS, LANES), 0)
    for position, total in enumerate(totals):
        whole = jnp.sum(jnp.sum(total, axis=0, keepdims=True), axis=1, keepdims=True)
        found.append((position + 1, jnp.where(line == 0, whole, 0.0)))
    sums[...] = in_sums(found)
    gather(sums, sums_out, refs[0], refs[1])


def update_kernel(later, final, *refs):
    inverse, gathered, ext, weights, solution, residual, image = refs[:7]
    refs = refs[7:]
    if later:
        direction, direction_image, scalars = refs[:3]
        refs = refs[3:]
    solution_out, residual_out = refs[:2]
    refs = refs[2:]
    if not final:
        direction_out, direction_image_out, scalars_out, image_out, sums_out = refs[:5]
        refs = refs[5:]
        greet()
    values, spread = refs[:2]
    rows_axial, rows_circ, depth = solution.shape
    values[...] = jnp.dot(inverse[...], gathered[...], precision=PRECISE)
    spread_into(spread, values, 0, ext.at[2])
    totals = jnp.sum(gathered[...], axis=0, keepdims=True)
    norm = totals[:, 1:2]
    overlap = jnp.sum(gathered[...] * values[...], axis=0, keepdims=True)[:, 0:1]
    curvature = totals[:, 2:3] - overlap
    if later:
        ratio = norm / scalars[0:1, 0:1]
        curvature = ratio * ratio * scalars[0:1, 1:2] + 2.0 * ratio * totals[:, 3:4] + curvature
    step = norm / curvature

    def plane(x, carry):
        now = residual[x]
        along = now - window_of(spread, x, rows_circ, (0, 0))
        along_image = image[x] - apply_plane(spread, weights, x, rows_circ)
        if later:
            along = along + ratio * direction[x]
            along_image = along_image + ratio * direction_image[x]
        solution_out[x] = solution[x] + step * along
        residual_out[x] = now - step * along_image
        if not final:
            direction_out[x] = along
            direction_image_out[x] = along_image
        return carry

    lax.fori_loop(0, rows_axial, plane, 0)
    if not final:
        scalars_out[...] = in_sums([(0, norm), (1, curvature)])
        field, sums = refs[2:4]
        image_sums(
            residual_out, field, ext, weights, direction_image_out, image_out, sums, sums_out, refs[4:]
        )


def call(kernel, outs, scratch, args, name, collective_id=None):
    return pl.pallas_call(
        kernel,
        out_shape=[jax.ShapeDtypeStruct(shape, jnp.float32) for shape in outs],
        in_specs=[VMEM] * len(args),
        out_specs=[VMEM] * len(outs),
        scratch_shapes=[
            pltpu.VMEM(shape, jnp.float32) if isinstance(shape, tuple) else shape for shape in scratch
        ],
        compiler_params=params(collective_id),
        name=name,
    )(*args)


def shards(right_side, stiffness, material, groups):
    block = right_side.shape
    rows_axial, rows_circ, depth = block
    devices = lax.axis_size("axial") * lax.axis_size("circ")
    padded = (rows_axial + 2, rows_circ + 2 * PAD, depth)
    count = 2 * len(HALF_STEPS) + 1
    tile = (LABELS, LANES)
    tiles = (devices,) + tile
    flat = (devices * LABELS, LANES)
    size = LABELS * rows_circ
    pair = [pltpu.SemaphoreType.DMA, pltpu.SemaphoreType.DMA]
    ext, weights, gathered = call(
        weights_kernel,
        [(3,) + padded, (count,) + block, tiles],
        [tile, (len(HALF_STEPS),) + padded, (count, rows_circ, depth), (len(PANELS), size, size)]
        + pair
        + halo_buffers(3, block),
        [stiffness, material, groups, right_side],
        "weights",
        0,
    )
    gathered = gathered.reshape(flat)
    inverse = coarse_inverse(gathered)
    work = [flat, padded]
    talk = [(1,) + padded, tile] + pair + halo_buffers(1, block)
    solution, residual, image, sums = call(
        start_kernel,
        [block, block, block, tiles],
        work + talk,
        [inverse, gathered, ext, weights, right_side],
        "start",
        1,
    )
    carried = []
    for iteration in range(ITERS):
        later, final = iteration > 0, iteration + 1 == ITERS
        outs = [block, block] + ([] if final else [block, block, tile, block, tiles])
        solution, residual, *carried = call(
            functools.partial(update_kernel, later, final),
            outs,
            work + ([] if final else talk),
            [inverse, sums.reshape(flat), ext, weights, solution, residual, image] + carried,
            "update",
            None if final else 2 + iteration,
        )
        if not final:
            image, sums = carried[3:]
            carried = carried[:3]
    return (solution, residual)


def solution(mesh):
    in_specs = (
        P("axial", "circ", None),
        P("axial", "circ", None),
        P("axial", "circ", None),
        P("axial", "circ", None),
    )
    out_specs = (P("axial", "circ", None), P("axial", "circ", None))
    return jax.shard_map(shards, mesh=mesh, in_specs=in_specs, out_specs=out_specs, check_vma=False)
```

```python
import functools
import math

import jax
import jax.numpy as jnp
from jax import lax
from jax.experimental import pallas as pl
from jax.experimental.pallas import tpu as pltpu
from jax.sharding import PartitionSpec as P

LABELS = 8
ITERS = 2
MASS_SHIFT = 0.02
PRECISE = lax.Precision.HIGHEST
MESH = pl.DeviceIdType.MESH
PAD = 8
LANES = 128
VMEM = pl.BlockSpec(memory_space=pltpu.VMEM)
HALF_STEPS = (
    (0, 0, 1),
    (0, 1, -1),
    (0, 1, 0),
    (0, 1, 1),
    (1, -1, -1),
    (1, -1, 0),
    (1, -1, 1),
    (1, 0, -1),
    (1, 0, 0),
    (1, 0, 1),
    (1, 1, -1),
    (1, 1, 0),
    (1, 1, 1),
)


SIDES = tuple((a, c) for a in (-1, 0, 1) for c in (-1, 0, 1) if (a, c) != (0, 0))
PANELS = ((0, 0), (0, 1), (1, -1), (1, 0), (1, 1))


def params(collective_id=None):
    if collective_id is None:
        return pltpu.CompilerParams(vmem_limit_bytes=56 * 1024 * 1024)
    return pltpu.CompilerParams(
        vmem_limit_bytes=56 * 1024 * 1024, collective_id=collective_id, has_side_effects=True
    )


def wrapped(value, length):
    return value - jnp.where(value >= length, length, 0)


def for_others(action):
    axials, circs = lax.axis_size("axial"), lax.axis_size("circ")
    for c in range(1, circs):
        action(0, c)

    def row(a, carry):
        for c in range(circs):
            action(a, c)
        return carry

    lax.fori_loop(1, axials, row, 0)


def other(a, c):
    axials, circs = lax.axis_size("axial"), lax.axis_size("circ")
    return (
        wrapped(lax.axis_index("axial") + a, axials),
        wrapped(lax.axis_index("circ") + c, circs),
    )


def greet():
    barrier = pltpu.get_barrier_semaphore()

    def signal(a, c):
        pl.semaphore_signal(barrier, inc=1, device_id=other(a, c), device_id_type=MESH)

    for_others(signal)


def greeted():
    devices = lax.axis_size("axial") * lax.axis_size("circ")
    pl.semaphore_wait(pltpu.get_barrier_semaphore(), devices - 1)


def inside(move):
    at = lax.axis_index("axial") + move
    return jnp.logical_and(at >= 0, at < lax.axis_size("axial"))


def halo_buffers(count, block):
    rows_axial, rows_circ, depth = block
    buffers = [
        pltpu.VMEM((2, count, rows_axial, depth), jnp.float32),
        pltpu.VMEM((2, count, rows_circ, depth), jnp.float32),
        pltpu.VMEM((4, count, 1, depth), jnp.float32),
    ]
    return buffers + buffers + [pltpu.SemaphoreType.DMA((len(SIDES),))] * 2


def halo_copy(side, refs):
    send_circ, send_axial, send_corner, recv_circ, recv_axial, recv_corner, send_sem, recv_sem = refs
    circs = lax.axis_size("circ")
    a, c = (side[0] + 1) // 2, (side[1] + 1) // 2
    if side[0] == 0:
        source, target = send_circ.at[c], recv_circ.at[1 - c]
    elif side[1] == 0:
        source, target = send_axial.at[a], recv_axial.at[1 - a]
    else:
        source, target = send_corner.at[2 * a + c], recv_corner.at[3 - 2 * a - c]
    number = SIDES.index(side)
    return pltpu.make_async_remote_copy(
        src_ref=source,
        dst_ref=target,
        send_sem=send_sem.at[number],
        recv_sem=recv_sem.at[number],
        device_id=(
            lax.axis_index("axial") + side[0],
            wrapped(lax.axis_index("circ") + side[1] % circs, circs),
        ),
        device_id_type=MESH,
    )


def halo_send(fields, refs):
    send_circ, send_axial, send_corner = refs[:3]
    rows_axial, rows_circ, depth = fields[0].shape
    for f, field in enumerate(fields):
        for a in range(2):
            x = a * (rows_axial - 1)
            send_axial[a, f] = field[x].astype(jnp.float32)
            for c in range(2):
                row = c * (rows_circ - 1)
                send_corner[2 * a + c, f] = field[x, row : row + 1, :].astype(jnp.float32)
        for c in range(2):
            row = c * (rows_circ - 1)
            for x in range(rows_axial):
                send_circ[c, f, x : x + 1, :] = field[x, row : row + 1, :].astype(jnp.float32)
    greeted()
    for side in SIDES:
        @pl.when(inside(side[0]))
        def _():
            halo_copy(side, refs).start()


def halo_fill(fields, out):
    rows_axial, rows_circ, depth = fields[0].shape
    for f, field in enumerate(fields):
        for x in (0, rows_axial + 1):
            out[f, x] = jnp.zeros((rows_circ + 2 * PAD, depth), jnp.float32)
        blank = jnp.zeros((rows_axial, PAD, depth), jnp.float32)
        out[f, 1 : rows_axial + 1, 0:PAD, :] = blank
        out[f, 1 : rows_axial + 1, PAD + rows_circ :, :] = blank
        out[f, 1 : rows_axial + 1, PAD : PAD + rows_circ, :] = field[...].astype(jnp.float32)


def halo_receive(fields, out, refs):
    recv_circ, recv_axial, recv_corner = refs[3:6]
    rows_axial, rows_circ, depth = fields[0].shape
    count = len(fields)
    edge = (PAD - 1, PAD + rows_circ)
    for side in SIDES:
        a, c = (1 - side[0]) // 2, (1 - side[1]) // 2
        x = a * (rows_axial + 1)

        @pl.when(inside(-side[0]))
        def _():
            halo_copy(side, refs).wait_recv()
            for f in range(count):
                if side[0] == 0:
                    for row in range(rows_axial):
                        out[f, row + 1, edge[c] : edge[c] + 1, :] = recv_circ[c, f, row : row + 1, :]
                elif side[1] == 0:
                    out[f, x, PAD : PAD + rows_circ, :] = recv_axial[a, f]
                else:
                    out[f, x, edge[c] : edge[c] + 1, :] = recv_corner[2 * a + c, f]

    for side in SIDES:
        @pl.when(inside(side[0]))
        def _():
            halo_copy(side, refs).wait_send()


def gather(own, out, send_sem, recv_sem):
    axials, circs = lax.axis_size("axial"), lax.axis_size("circ")
    me = lax.axis_index("axial") * circs + lax.axis_index("circ")

    def send(a, c):
        pltpu.make_async_remote_copy(
            src_ref=own,
            dst_ref=out.at[me],
            send_sem=send_sem,
            recv_sem=recv_sem,
            device_id=other(a, c),
            device_id_type=MESH,
        ).start()

    for_others(send)
    out[me] = own[...]
    most = out.at[pl.ds(0, axials * circs - 1)]
    everything = pltpu.make_async_remote_copy(
        src_ref=most,
        dst_ref=most,
        send_sem=send_sem,
        recv_sem=recv_sem,
        device_id=other(0, 1),
        device_id_type=MESH,
    )
    everything.wait_recv()
    everything.wait_send()


def shifted(window, move):
    if move == 0:
        return window
    depth = window.shape[-1]
    lane = lax.broadcasted_iota(jnp.int32, window.shape, window.ndim - 1)
    rolled = pltpu.roll(window, (depth - move) % depth, window.ndim - 1)
    return jnp.where(lane == (depth - 1 if move > 0 else 0), 0.0, rolled)


def window_of(ref, x, rows_circ, offset):
    return ref[x + 1 + offset[0], PAD + offset[1] : PAD + offset[1] + rows_circ, :]


def opposite(offset):
    return (-offset[0], -offset[1], -offset[2])


def terms():
    listed = []
    for position, offset in enumerate(HALF_STEPS):
        listed.append((position, offset))
        listed.append((len(HALF_STEPS) + position, opposite(offset)))
    return sorted(listed, key=lambda term: term[1])


def in_sums(sums):
    lane = lax.broadcasted_iota(jnp.int32, (LABELS, LANES), 1)
    tile = jnp.zeros((LABELS, LANES), jnp.float32)
    for position, value in sums:
        tile = tile + jnp.where(lane == position, value, 0.0)
    return tile


def label_sums(groups_ref, field_of, rows_axial, rows_circ, depth):
    def plane(x, sums):
        labels = window_of(groups_ref, x, rows_circ, (0, 0))
        value = field_of(x)
        return tuple(
            total + jnp.where(labels == float(label), value, 0.0)
            for label, total in enumerate(sums)
        )

    blank = jnp.zeros((rows_circ, depth), jnp.float32)
    sums = lax.fori_loop(0, rows_axial, plane, (blank,) * LABELS)
    rows = [jnp.sum(total, axis=0, keepdims=True) for total in sums]
    return jnp.sum(jnp.concatenate(rows, axis=0), axis=1, keepdims=True)


def weights_kernel(stiffness, material_ref, groups_ref, right, ext, weights, gathered, panel, stiff, seen, gather_send, gather_recv, *halo_refs):
    rows_axial, rows_circ, depth = right.shape
    greet()
    fields = (stiffness, material_ref, groups_ref)
    halo_send(fields, halo_refs)
    halo_fill(fields, ext)
    own = label_sums(ext.at[2], lambda x: right[x], rows_axial, rows_circ, depth)
    halo_receive(fields, ext, halo_refs)
    groups = ext.at[2]
    half = len(HALF_STEPS)

    def stiffness_plane(x, carry):
        scale = ext[0, x]
        material = ext[1, x]
        upper = material >= 8.0
        angle = material - jnp.where(upper, 8.0, 0.0)
        first = jnp.full_like(scale, 1.0)
        second = jnp.zeros_like(scale)
        for turn in range(1, 8):
            first = jnp.where(angle == float(turn), math.cos(math.pi * turn / 8.0), first)
            second = jnp.where(angle == float(turn), math.sin(math.pi * turn / 8.0), second)
        shrink = jnp.where(upper, 0.6, 1.0)
        first, second = first * shrink, second * shrink
        third = jnp.where(upper, 0.8, 0.0)
        flat = scale * jnp.where(upper, 0.35 * 0.15, 0.15)
        along = scale * jnp.where(upper, 0.35 * 2.0, 6.0)
        for position, offset in enumerate(HALF_STEPS):
            length = float(sum(part * part for part in offset))
            dot = None
            for part, line in zip(offset, (first, second, third)):
                if part != 0:
                    line = line if part > 0 else -line
                    dot = line if dot is None else dot + line
            stiff[position, x] = flat * (1.0 / length) + along * (dot * dot) * (1.0 / (length * length))
        return carry

    lax.fori_loop(0, rows_axial + 2, stiffness_plane, 0)

    def weight_plane(x, carry):
        diagonal = None
        for position, offset in enumerate(HALF_STEPS):
            field = stiff.at[position]
            centre = window_of(field, x, rows_circ, (0, 0))
            ahead = 0.5 * (centre + shifted(window_of(field, x, rows_circ, offset), offset[2]))
            back = opposite(offset)
            behind = 0.5 * (centre + shifted(window_of(field, x, rows_circ, back), back[2]))
            weights[position, x] = ahead
            weights[half + position, x] = behind
            pair = ahead + behind
            diagonal = pair if diagonal is None else diagonal + pair
        weights[2 * half, x] = MASS_SHIFT + diagonal
        return carry

    lax.fori_loop(0, rows_axial, weight_plane, 0)

    row = lax.broadcasted_iota(jnp.int32, (rows_circ, depth), 0)
    last = rows_axial - 1

    def one_hot(labels):
        return jnp.concatenate(
            [jnp.where(labels == float(label), 1.0, 0.0) for label in range(LABELS)], axis=0
        )

    def moved(labels, move):
        if move == 0:
            return labels
        lane = lax.broadcasted_iota(jnp.int32, labels.shape, 1)
        rolled = pltpu.roll(labels, (depth - move) % depth, 1)
        return jnp.where(lane == (depth - 1 if move > 0 else 0), -1.0, rolled)

    def seen_labels(offset, x):
        return moved(window_of(groups, x, rows_circ, offset), offset[2])

    def pair_sums(labels, parts):
        return lax.dot_general(
            one_hot(labels),
            jnp.concatenate(parts, axis=0),
            (((1,), (1,)), ((), ())),
            precision=PRECISE,
            preferred_element_type=jnp.float32,
        )

    def panel_plane(x, total):
        for position, offset in enumerate(HALF_STEPS):
            labels = seen_labels(offset, x)
            if offset[0] != 0:
                labels = jnp.where(x == last, -1.0, labels)
            if offset[1] != 0:
                leaves = row == (rows_circ - 1 if offset[1] > 0 else 0)
                labels = jnp.where(leaves, -1.0, labels)
            seen[position] = labels
        parts = []
        for label in range(LABELS):
            found = jnp.zeros((rows_circ, depth), jnp.float32)
            for position in range(half):
                found = found - jnp.where(seen[position] == float(label), weights[position, x], 0.0)
            parts.append(found)
        return total + pair_sums(window_of(groups, x, rows_circ, (0, 0)), parts)

    size = LABELS * rows_circ
    totals = [lax.fori_loop(0, rows_axial, panel_plane, jnp.zeros((size, size), jnp.float32))]

    plane = lax.broadcasted_iota(jnp.int32, (rows_axial, depth), 0)
    chosen = []
    for position, offset in terms():
        if offset[1] > 0:
            first = 1 + offset[0]
            labels = moved(groups[first : first + rows_axial, PAD + rows_circ, :], offset[2])
            if offset[0] != 0:
                labels = jnp.where(plane == (last if offset[0] > 0 else 0), -1.0, labels)
            chosen.append((labels, weights[position, :, rows_circ - 1, :]))

    def panel_of(chosen, shape):
        parts = []
        for label in range(LABELS):
            found = jnp.zeros(shape, jnp.float32)
            for labels, weight in chosen:
                found = found - jnp.where(labels == float(label), weight, 0.0)
            parts.append(found)
        return parts

    beside = groups[1 : 1 + rows_axial, PAD + rows_circ - 1, :]
    totals.append(pair_sums(beside, panel_of(chosen, (rows_axial, depth))))

    for slot in range(2, len(PANELS)):
        move = PANELS[slot][1]
        chosen = []
        for position, offset in enumerate(HALF_STEPS):
            if offset[0] > 0 and (offset[1] == move or move == 0):
                labels = seen_labels(offset, last)
                if offset[1] != 0:
                    leaves = row == (rows_circ - 1 if offset[1] > 0 else 0)
                    labels = jnp.where(leaves == (move != 0), labels, -1.0)
                chosen.append((labels, weights[position, last]))
        centre = window_of(groups, last, rows_circ, (0, 0))
        totals.append(pair_sums(centre, panel_of(chosen, (rows_circ, depth))))

    result = jnp.zeros((LABELS, LANES), jnp.float32)
    for slot, total in enumerate(totals):
        size = total.shape[0]
        rows = size // LABELS
        line = lax.broadcasted_iota(jnp.int32, (size, size), 0)
        column = lax.broadcasted_iota(jnp.int32, (size, size), 1)
        same = lax.rem(line, rows) == lax.rem(column, rows)
        tile_row = lax.broadcasted_iota(jnp.int32, (LABELS, size), 0)
        tile_column = lax.broadcasted_iota(jnp.int32, (LABELS, size), 1)
        collect = jnp.where(tile_column // rows == tile_row, 1.0, 0.0)
        spot_row = lax.broadcasted_iota(jnp.int32, (size, LANES), 0)
        spot_column = lax.broadcasted_iota(jnp.int32, (size, LANES), 1)
        spots = jnp.where(spot_row // rows + slot * LABELS == spot_column, 1.0, 0.0)
        lines = jnp.dot(collect, jnp.where(same, total, 0.0), precision=PRECISE)
        result = result + jnp.dot(lines, spots, precision=PRECISE)
    centre = label_sums(groups, lambda x: weights[2 * half, x], rows_axial, rows_circ, depth)
    spot_row = lax.broadcasted_iota(jnp.int32, (LABELS, LANES), 0)
    spot_column = lax.broadcasted_iota(jnp.int32, (LABELS, LANES), 1)
    result = result + jnp.where(spot_row == spot_column, 0.5 * centre, 0.0)
    panel[...] = result + in_sums([(len(PANELS) * LABELS, own)])
    gather(panel, gathered, gather_send, gather_recv)


def inverse_two(a, b, c):
    scale = 1.0 / (a * c - b * b)
    return c * scale, -b * scale, a * scale


def inverse_four(e):
    a, b, c = inverse_two(e[0][0], e[1][0], e[1][1])
    q = ((e[2][0], e[3][0]), (e[2][1], e[3][1]))
    t = [[a * q[0][k] + b * q[1][k] for k in range(2)], [b * q[0][k] + c * q[1][k] for k in range(2)]]

    def rest(i, k):
        return e[2 + max(i, k)][2 + min(i, k)] - (q[0][i] * t[0][k] + q[1][i] * t[1][k])

    x, y, z = inverse_two(rest(0, 0), rest(0, 1), rest(1, 1))
    u = [[t[i][0] * x + t[i][1] * y, t[i][0] * y + t[i][1] * z] for i in range(2)]

    def corner(i, k):
        return u[i][0] * t[k][0] + u[i][1] * t[k][1]

    across = b + corner(0, 1)
    return [
        [a + corner(0, 0), across, -u[0][0], -u[0][1]],
        [across, c + corner(1, 1), -u[1][0], -u[1][1]],
        [-u[0][0], -u[1][0], x, y],
        [-u[0][1], -u[1][1], y, z],
    ]


def inverse_of(matrices):
    size = matrices[0].shape[0]
    tiles = size // 8
    values = [matrix.reshape(tiles, 8, size) for matrix in matrices]
    lane = lax.broadcasted_iota(jnp.int32, (1, 8, size), 2)
    line = lax.broadcasted_iota(jnp.int32, (1, 8, size), 1)
    wide = (tiles, 8, size)
    for first in range(0, size, 4):
        tile, sub = first // 8, first % 8
        for number, value in enumerate(values):
            columns = [
                jnp.broadcast_to(value[:, :, first + k : first + k + 1], wide) for k in range(4)
            ]
            entries = [
                [
                    jnp.broadcast_to(columns[k][tile : tile + 1, sub + i : sub + i + 1, :], (1, 8, size))
                    for k in range(i + 1)
                ]
                for i in range(4)
            ]
            rows = []
            for i in range(4):
                row = jnp.broadcast_to(value[tile : tile + 1, sub + i : sub + i + 1, :], (1, 8, size))
                for k in range(4):
                    row = jnp.where(lane == first + k, 1.0 if i == k else 0.0, row)
                rows.append(row)
            small = inverse_four(entries)
            fresh = [
                (small[i][0] * rows[0] + small[i][1] * rows[1])
                + (small[i][2] * rows[2] + small[i][3] * rows[3])
                for i in range(4)
            ]
            inside = jnp.logical_and(lane >= first, lane < first + 4)
            left = jnp.where(inside, 0.0, value)
            left = (left - columns[0] * fresh[0] - columns[1] * fresh[1]) - (
                columns[2] * fresh[2] + columns[3] * fresh[3]
            )
            own = left[tile : tile + 1]
            for i in range(4):
                own = jnp.where(line == sub + i, fresh[i], own)
            parts = [left[:tile]] * (tile > 0) + [own] + [left[tile + 1 :]] * (tile + 1 < tiles)
            values[number] = jnp.concatenate(parts, axis=0)
    return [value.reshape(size, size) for value in values]


def coarse_kernel(cycles, gathered, inverse, diagonals, uppers, held, linked, partial):
    size = gathered.shape[0] // cycles
    whole = gathered.shape[0]
    circs = size // LABELS
    spread_row = lax.broadcasted_iota(jnp.int32, (LANES, size), 0)
    spread_column = lax.rem(lax.broadcasted_iota(jnp.int32, (LANES, size), 1), LABELS)
    line = lax.rem(lax.broadcasted_iota(jnp.int32, (whole, size), 0) // LABELS, circs)
    column = lax.broadcasted_iota(jnp.int32, (whole, size), 1) // LABELS

    def dot(left, right):
        return jnp.dot(left, right, precision=PRECISE, preferred_element_type=jnp.float32)

    def blocks(slot):
        tiles = jnp.where(spread_row == spread_column + slot * LABELS, 1.0, 0.0)
        placed = dot(gathered[...], tiles)
        return jnp.where(lax.rem(line + PANELS[slot][1] + circs, circs) == column, placed, 0.0)

    own = blocks(0) + blocks(1)
    ahead = blocks(2) + blocks(3) + blocks(4)
    for s in range(cycles):
        part = own[s * size : (s + 1) * size]
        diagonals[s] = part + part.T
        uppers[s] = ahead[s * size : (s + 1) * size]
    unit_line = lax.broadcasted_iota(jnp.int32, (size, whole), 0)
    unit_column = lax.broadcasted_iota(jnp.int32, (size, whole), 1)

    def unit(s):
        return jnp.where(unit_line + s * size == unit_column, 1.0, 0.0)

    def eliminate(s, s_next, upper):
        inverted = inverse_of([diagonals[s]])[0]
        link = dot(inverted, upper)
        held[s] = inverted
        linked[s] = link
        across = upper.T
        diagonals[s_next] = diagonals[s_next] - dot(across, link)
        partial[s_next] = partial[s_next] - dot(link.T, partial[s])

    def start(s, carry):
        partial[s] = unit(s)
        return carry

    lax.fori_loop(0, cycles, start, 0)
    middle = cycles // 2

    def from_both_ends(step, carry):
        low, high = step, cycles - 1 - step
        upper_low, upper_high = uppers[low], uppers[high - 1].T
        inverted_low, inverted_high = inverse_of([diagonals[low], diagonals[high]])
        for s, s_next, upper, inverted in (
            (low, low + 1, upper_low, inverted_low),
            (high, high - 1, upper_high, inverted_high),
        ):
            link = dot(inverted, upper)
            held[s] = inverted
            linked[s] = link
            diagonals[s_next] = diagonals[s_next] - dot(upper.T, link)
            partial[s_next] = partial[s_next] - dot(link.T, partial[s])
        return carry

    lax.fori_loop(0, middle - 1, from_both_ends, 0, unroll=whole <= 256)
    eliminate(middle - 1, middle, uppers[middle - 1])
    rows = pl.ds(middle * size, size)
    inverse[rows, :] = dot(inverse_of([diagonals[middle]])[0], partial[middle])

    def put(s, s_next):
        ahead = inverse[pl.ds(s_next * size, size), :]
        inverse[pl.ds(s * size, size), :] = dot(held[s], partial[s]) - dot(linked[s], ahead)

    put(middle - 1, middle)

    def back(step, carry):
        put(middle - 2 - step, middle - 1 - step)
        put(middle + 1 + step, middle + step)
        return carry

    lax.fori_loop(0, middle - 1, back, 0, unroll=whole <= 256)


def coarse_inverse(gathered):
    cycles, circs = lax.axis_size("axial"), lax.axis_size("circ")
    size, whole = circs * LABELS, gathered.shape[0]
    square = pltpu.VMEM((cycles, size, size), jnp.float32)
    return pl.pallas_call(
        functools.partial(coarse_kernel, cycles),
        out_shape=jax.ShapeDtypeStruct((whole, whole), jnp.float32),
        in_specs=[VMEM],
        out_specs=VMEM,
        scratch_shapes=[square] * 4 + [pltpu.VMEM((cycles, size, whole), jnp.float32)],
        compiler_params=params(),
        name="coarse_inverse",
    )(gathered)


def apply_plane(ext, weights, x, rows_circ):
    centre = 2 * len(HALF_STEPS)
    result = weights[centre, x] * window_of(ext, x, rows_circ, (0, 0))
    for position, offset in terms():
        value = shifted(window_of(ext, x, rows_circ, offset), offset[2])
        result = result - weights[position, x] * value
    return result


def spread_into(spread, values, column, groups):
    planes, rows, depth = spread.shape
    axials, circs = lax.axis_size("axial"), lax.axis_size("circ")
    axial, circ = lax.axis_index("axial"), lax.axis_index("circ")
    row = lax.broadcasted_iota(jnp.int32, (rows, depth), 0)

    def tile(a, c):
        at = axial + a
        present = jnp.logical_and(at >= 0, at < axials)
        at = jnp.minimum(jnp.maximum(at, 0), axials - 1)
        number = at * circs + lax.rem(circ + c + circs, circs)
        part = values[pl.ds(pl.multiple_of(number * LABELS, LABELS), LABELS), column : column + 1]
        return jnp.where(present, jnp.broadcast_to(part, (LABELS, depth)), 0.0)

    def fill(x, sides):
        labels = groups[x]
        value = jnp.zeros((rows, depth), jnp.float32)
        for label in range(LABELS):
            before, here, after = [side[label : label + 1, :] for side in sides]
            chosen = jnp.where(row < PAD, before, jnp.where(row < rows - PAD, here, after))
            value = jnp.where(labels == float(label), chosen, value)
        spread[x] = value

    fill(0, [tile(-1, c) for c in (-1, 0, 1)])
    fill(planes - 1, [tile(1, c) for c in (-1, 0, 1)])
    sides = [tile(0, c) for c in (-1, 0, 1)]

    def inner(x, carry):
        fill(x, sides)
        return carry

    lax.fori_loop(1, planes - 1, inner, 0)


def start_kernel(inverse, gathered, ext, weights, right, solution, residual, image, sums_out, *refs):
    values, spread, field, sums = refs[:4]
    rows_axial, rows_circ, depth = right.shape
    greet()
    values[...] = jnp.dot(inverse[...], gathered[...], precision=PRECISE)
    spread_into(spread, values, len(PANELS) * LABELS, ext.at[2])

    def plane(x, carry):
        solution[x] = window_of(spread, x, rows_circ, (0, 0))
        residual[x] = right[x] - apply_plane(spread, weights, x, rows_circ)
        return carry

    lax.fori_loop(0, rows_axial, plane, 0)
    image_sums(residual, field, ext, weights, None, image, sums, sums_out, refs[4:])


def image_sums(residual_ref, field_ext, ext, weights, direction_image, image, sums, sums_out, refs):
    later = direction_image is not None
    halo_send((residual_ref,), refs[2:])
    halo_fill((residual_ref,), field_ext)
    halo_receive((residual_ref,), field_ext, refs[2:])
    rows_axial, rows_circ, depth = image.shape
    field = field_ext.at[0]

    def plane(x, totals):
        value = apply_plane(field, weights, x, rows_circ)
        image[x] = value
        residual = window_of(field, x, rows_circ, (0, 0))
        factors = [residual, value] + ([direction_image[x]] if later else [])
        return tuple(total + residual * factor for total, factor in zip(totals, factors))

    blank = jnp.zeros((rows_circ, depth), jnp.float32)
    totals = lax.fori_loop(0, rows_axial, plane, (blank,) * (3 if later else 2))
    found = [(0, label_sums(ext.at[2], lambda x: image[x], rows_axial, rows_circ, depth))]
    line = lax.broadcasted_iota(jnp.int32, (LABELS, LANES), 0)
    for position, total in enumerate(totals):
        whole = jnp.sum(jnp.sum(total, axis=0, keepdims=True), axis=1, keepdims=True)
        found.append((position + 1, jnp.where(line == 0, whole, 0.0)))
    sums[...] = in_sums(found)
    gather(sums, sums_out, refs[0], refs[1])


def update_kernel(later, final, *refs):
    inverse, gathered, ext, weights, solution, residual, image = refs[:7]
    refs = refs[7:]
    if later:
        direction, direction_image, scalars = refs[:3]
        refs = refs[3:]
    solution_out, residual_out = refs[:2]
    refs = refs[2:]
    if not final:
        direction_out, direction_image_out, scalars_out, image_out, sums_out = refs[:5]
        refs = refs[5:]
        greet()
    values, spread = refs[:2]
    rows_axial, rows_circ, depth = solution.shape
    values[...] = jnp.dot(inverse[...], gathered[...], precision=PRECISE)
    spread_into(spread, values, 0, ext.at[2])
    totals = jnp.sum(gathered[...], axis=0, keepdims=True)
    norm = totals[:, 1:2]
    overlap = jnp.sum(gathered[...] * values[...], axis=0, keepdims=True)[:, 0:1]
    curvature = totals[:, 2:3] - overlap
    if later:
        ratio = norm / scalars[0:1, 0:1]
        curvature = ratio * ratio * scalars[0:1, 1:2] + 2.0 * ratio * totals[:, 3:4] + curvature
    step = norm / curvature

    def plane(x, carry):
        now = residual[x]
        along = now - window_of(spread, x, rows_circ, (0, 0))
        along_image = image[x] - apply_plane(spread, weights, x, rows_circ)
        if later:
            along = along + ratio * direction[x]
            along_image = along_image + ratio * direction_image[x]
        solution_out[x] = solution[x] + step * along
        residual_out[x] = now - step * along_image
        if not final:
            direction_out[x] = along
            direction_image_out[x] = along_image
        return carry

    lax.fori_loop(0, rows_axial, plane, 0)
    if not final:
        scalars_out[...] = in_sums([(0, norm), (1, curvature)])
        field, sums = refs[2:4]
        image_sums(
            residual_out, field, ext, weights, direction_image_out, image_out, sums, sums_out, refs[4:]
        )


def call(kernel, outs, scratch, args, name, collective_id=None):
    return pl.pallas_call(
        kernel,
        out_shape=[jax.ShapeDtypeStruct(shape, jnp.float32) for shape in outs],
        in_specs=[VMEM] * len(args),
        out_specs=[VMEM] * len(outs),
        scratch_shapes=[
            pltpu.VMEM(shape, jnp.float32) if isinstance(shape, tuple) else shape for shape in scratch
        ],
        compiler_params=params(collective_id),
        name=name,
    )(*args)


def shards(right_side, stiffness, material, groups):
    block = right_side.shape
    rows_axial, rows_circ, depth = block
    devices = lax.axis_size("axial") * lax.axis_size("circ")
    padded = (rows_axial + 2, rows_circ + 2 * PAD, depth)
    count = 2 * len(HALF_STEPS) + 1
    tile = (LABELS, LANES)
    tiles = (devices,) + tile
    flat = (devices * LABELS, LANES)
    pair = [pltpu.SemaphoreType.DMA, pltpu.SemaphoreType.DMA]
    ext, weights, gathered = call(
        weights_kernel,
        [(3,) + padded, (count,) + block, tiles],
        [tile, (len(HALF_STEPS),) + padded, (len(HALF_STEPS), rows_circ, depth)]
        + pair
        + halo_buffers(3, block),
        [stiffness, material, groups, right_side],
        "weights",
        0,
    )
    gathered = gathered.reshape(flat)
    inverse = coarse_inverse(gathered)
    work = [flat, padded]
    talk = [(1,) + padded, tile] + pair + halo_buffers(1, block)
    solution, residual, image, sums = call(
        start_kernel,
        [block, block, block, tiles],
        work + talk,
        [inverse, gathered, ext, weights, right_side],
        "start",
        1,
    )
    carried = []
    for iteration in range(ITERS):
        later, final = iteration > 0, iteration + 1 == ITERS
        outs = [block, block] + ([] if final else [block, block, tile, block, tiles])
        solution, residual, *carried = call(
            functools.partial(update_kernel, later, final),
            outs,
            work + ([] if final else talk),
            [inverse, sums.reshape(flat), ext, weights, solution, residual, image] + carried,
            "update",
            None if final else 2 + iteration,
        )
        if not final:
            image, sums = carried[3:]
            carried = carried[:3]
    return (solution, residual)


def solution(mesh):
    in_specs = (
        P("axial", "circ", None),
        P("axial", "circ", None),
        P("axial", "circ", None),
        P("axial", "circ", None),
    )
    out_specs = (P("axial", "circ", None), P("axial", "circ", None))
    return jax.shard_map(shards, mesh=mesh, in_specs=in_specs, out_specs=out_specs, check_vma=False)
```
